32 devices in a mesh: bevy: 4 (over y, x), bevx: 4 (over z), cam: 2 (over core).
Axes of the slice: x: 2, y: 2, z: 4, core: 2. Of those that a mesh axis runs over, the one named last changes fastest.
Arguments:
- image_tokens: bfloat16 [8192, 768], P(('bevy', 'bevx', 'cam')), may hold values from -6 to 6
- lift_weight: bfloat16 [768, 1024], replicated, may hold values from -0.21875 to 0.21875
- route_token: int32 [16, 2, 16, 8], P(('bevy', 'bevx'), 'cam'), may hold values from 0 to 255
- route_cell: int32 [16, 2, 16, 8], P(None, 'cam', ('bevy', 'bevx')), may hold values from 0 to 1023
- slot_counts: int32 [16, 2, 16], P(('bevy', 'bevx'), 'cam'), may hold values from 0 to 8, as said below
- norm_gain: float32 [1024], replicated, may hold values from 0.1 to 1.9
- w_query: bfloat16 [1024, 1024], replicated, may hold values from -0.1875 to 0.1875
- w_key: bfloat16 [1024, 1024], replicated, may hold values from -0.1875 to 0.1875
- w_value: bfloat16 [1024, 1024], replicated, may hold values from -0.1875 to 0.1875
- w_out: bfloat16 [1024, 1024], replicated, may hold values from -0.1875 to 0.1875
- key_bias: bfloat16 [64, 256, 16], P(None, 'bevx'), may hold values from -1.5 to 260
Outputs:
- bev_out: bfloat16 [64, 256, 1024], P(('bevy', 'cam'), 'bevx')
The draws below stay inside these ranges and needn't reach their ends.
Inputs may be any that keep to these rules, and one draw needn't show every extreme that they name: The first slot_counts slots of a source device and tile are live; at most 8. In every draw some tile receives 8 live slots from every source device.
All inputs are finite; a program needn't handle non-finite values.
Results may differ from the reference program's by a relative error of at most 0.0055.
Values may be sent and summed in bfloat16 or wider, within the bound.
A program may use at most 128 MiB of HBM per device.

```python
import jax
import jax.numpy as jnp
from jax import lax

IN_W = 768
D = 1024
HEADS = 16
HEAD_DIM = 64
TOK_DEV = 256
SLOT = 8
ROWS_DEV = 8
COLS_DEV = 64
HALO = 4
TILES = 16
CELLS = 1024
GRID_R = 64
GRID_C = 256
TOKENS = 8192
N_BEVY = 4
N_BEVX = 4
N_CAM = 2


def draw_slot_counts(key, part):
    first, second, third, fourth = jax.random.split(key, 4)
    shape_all = (TILES, N_CAM, TILES)
    ceiling = jax.random.randint(first, (1, 1, TILES), SLOT // 4, SLOT + 1)
    base_counts = jnp.minimum(jax.random.randint(second, shape_all, 0, SLOT + 1), ceiling)
    hot_source = jax.random.randint(third, (TILES, N_CAM, 1), 0, TILES)
    hot_tile = jax.random.randint(fourth, (), 0, TILES)
    tile_ids = lax.broadcasted_iota(jnp.int32, shape_all, 2)
    filled = (tile_ids == hot_source) | (tile_ids == hot_tile)
    return jnp.where(filled, SLOT, base_counts).astype(jnp.int32)


def peak_mask(row_key, col_key, on_key):
    block_rows = GRID_R // ROWS_DEV
    block_cols = GRID_C // COLS_DEV
    block_shape = (block_rows, 1, block_cols, 1, HEADS)
    full_shape = (block_rows, ROWS_DEV, block_cols, COLS_DEV, HEADS)
    peak_row = jax.random.randint(row_key, block_shape, 0, ROWS_DEV)
    peak_col = jax.random.randint(col_key, block_shape, 0, COLS_DEV)
    peak_on = jax.random.bernoulli(on_key, 0.5, block_shape)
    row_inside = lax.broadcasted_iota(jnp.int32, full_shape, 1)
    col_inside = lax.broadcasted_iota(jnp.int32, full_shape, 3)
    chosen = peak_on & (row_inside == peak_row) & (col_inside == peak_col)
    return chosen.reshape(GRID_R, GRID_C, HEADS)


def draw_key_bias(key, part):
    first, second, third, fourth = jax.random.split(key, 4)
    shape_all = (GRID_R, GRID_C, HEADS)
    peaks = peak_mask(second, third, fourth)
    flat_bias = jax.random.uniform(first, shape_all, jnp.float32, -1.0, 1.0)
    return jnp.where(peaks, 6.0, flat_bias).astype(jnp.bfloat16)


def set_ends(values, rng, least, largest):
    place = [jax.random.randint(jax.random.fold_in(rng, axis), (), 0, length) for axis, length in enumerate(values.shape)]
    longest = values.shape.index(max(values.shape))
    neighbour = place[:longest] + [(place[longest] + 1) % values.shape[longest]] + place[longest + 1:]
    return values.at[tuple(place)].set(least).at[tuple(neighbour)].set(largest)


def block_scale(own_key, shape, cuts, low, top_value):
    gain, own = 1.0, jax.random.fold_in(own_key, 6)
    for dim, parts in cuts:
        heights = jnp.exp(jax.random.uniform(jax.random.fold_in(own, dim), (parts,), jnp.float32, low / len(cuts), top_value / len(cuts)))
        gain = gain * jnp.repeat(heights, shape[dim] // parts).reshape([-1 if axis == dim else 1 for axis in range(len(shape))])
    return gain


def scatter_about(rng, shape, width, reach, cuts=(), kind=jnp.bfloat16):
    gain = block_scale(rng, shape, cuts, -0.22, 0.18) if cuts else 1.0
    entries = jax.random.normal(rng, shape, jnp.float32) * width * gain
    return jnp.minimum(jnp.maximum(entries, -reach), reach).astype(kind)


def setup_inputs(seed: int = 0) -> dict:
    seeds = jax.random.split(jax.random.key(seed), 12)
    return {
        "image_tokens": scatter_about(seeds[0], (TOKENS, IN_W), 1.0, 6.0, ((0, 32),)),
        "lift_weight": scatter_about(seeds[1], (IN_W, D), IN_W ** -0.5, 0.21875),
        "route_token": set_ends(jax.random.randint(seeds[2], (TILES, N_CAM, TILES, SLOT), 0, TOK_DEV), jax.random.fold_in(seeds[2], 1), 0, TOK_DEV - 1).astype(jnp.int32),
        "route_cell": set_ends(jax.random.randint(seeds[3], (TILES, N_CAM, TILES, SLOT), 0, CELLS), jax.random.fold_in(seeds[3], 1), 0, CELLS - 1).astype(jnp.int32),
        "slot_counts": draw_slot_counts(jax.random.fold_in(seeds[11], 71), 0),
        "norm_gain": jnp.clip(1.0 + 0.18 * jax.random.normal(seeds[5], (D,), jnp.float32), 0.1, 1.9),
        "w_query": scatter_about(seeds[6], (D, D), D ** -0.5, 0.1875),
        "w_key": scatter_about(seeds[7], (D, D), D ** -0.5, 0.1875),
        "w_value": scatter_about(seeds[8], (D, D), D ** -0.5, 0.1875),
        "w_out": scatter_about(seeds[9], (D, D), D ** -0.5, 0.1875),
        "key_bias": draw_key_bias(jax.random.fold_in(seeds[11], 71), 0),
    }


def reference(image_tokens, lift_weight, route_token, route_cell, slot_counts, norm_gain, w_query, w_key, w_value, w_out, key_bias):
    tile_count = N_BEVY * N_BEVX
    projected = jnp.dot(image_tokens, lift_weight, preferred_element_type=jnp.float32).astype(jnp.bfloat16)
    source_base = (jnp.arange(tile_count, dtype=jnp.int32)[:, None] * N_CAM + jnp.arange(N_CAM, dtype=jnp.int32)[None, :]) * TOK_DEV
    global_index = (source_base[:, :, None, None] + route_token).astype(jnp.int32)
    is_live = jnp.arange(SLOT, dtype=jnp.int32)[None, None, None, :] < slot_counts[..., None]

    def lift_tile(tile_index):
        token_ids = global_index[:, :, tile_index, :].reshape(-1)
        live_now = is_live[:, :, tile_index, :].reshape(-1)
        cell_index = route_cell[:, :, tile_index, :].reshape(-1)
        slot_rows = jnp.where(live_now[:, None], projected[token_ids].astype(jnp.float32), jnp.float32(0.0))
        return jax.ops.segment_sum(slot_rows, cell_index, num_segments=CELLS)
    tile_sums = lax.map(lift_tile, jnp.arange(tile_count, dtype=jnp.int32))
    lifted = tile_sums.reshape(N_BEVY, N_BEVX, N_CAM * ROWS_DEV, COLS_DEV, D)
    lifted = lifted.transpose(0, 2, 1, 3, 4).reshape(GRID_R, GRID_C, D)
    mean_square = lax.optimization_barrier(jnp.mean(lifted * lifted, axis=-1, keepdims=True))
    normed = (lifted * lax.rsqrt(mean_square + 1e-06) * norm_gain).astype(jnp.bfloat16)
    flat_normed = normed.reshape(-1, D)
    queries = jnp.dot(flat_normed, w_query, preferred_element_type=jnp.float32).astype(jnp.bfloat16).reshape(GRID_R, GRID_C, D)
    key_vectors = jnp.dot(flat_normed, w_key, preferred_element_type=jnp.float32).astype(jnp.bfloat16).reshape(GRID_R, GRID_C, D)
    value_vectors = jnp.dot(flat_normed, w_value, preferred_element_type=jnp.float32).astype(jnp.bfloat16).reshape(GRID_R, GRID_C, D)
    pad_rows = ((HALO, HALO), (0, 0), (0, 0))
    key_padded = jnp.pad(key_vectors, pad_rows)
    value_padded = jnp.pad(value_vectors, pad_rows)
    bias_padded = jnp.pad(key_bias, pad_rows)
    window_count = GRID_C // COLS_DEV
    block_count = GRID_R // ROWS_DEV
    score_scale = HEAD_DIM ** (-0.5)

    def window_block(block_index):
        first_row = (block_index * ROWS_DEV).astype(jnp.int32)
        query_block = lax.dynamic_slice_in_dim(queries, first_row, ROWS_DEV, 0)
        key_block = lax.dynamic_slice_in_dim(key_padded, first_row, 2 * ROWS_DEV, 0)
        value_block = lax.dynamic_slice_in_dim(value_padded, first_row, 2 * ROWS_DEV, 0)
        bias_block = lax.dynamic_slice_in_dim(bias_padded, first_row, 2 * ROWS_DEV, 0)
        query_win = query_block.reshape(ROWS_DEV, window_count, COLS_DEV, HEADS, HEAD_DIM).transpose(1, 0, 2, 3, 4).reshape(window_count, ROWS_DEV * COLS_DEV, HEADS, HEAD_DIM)
        key_win = key_block.reshape(2 * ROWS_DEV, window_count, COLS_DEV, HEADS, HEAD_DIM).transpose(1, 0, 2, 3, 4).reshape(window_count, 2 * ROWS_DEV * COLS_DEV, HEADS, HEAD_DIM)
        value_win = value_block.reshape(2 * ROWS_DEV, window_count, COLS_DEV, HEADS, HEAD_DIM).transpose(1, 0, 2, 3, 4).reshape(window_count, 2 * ROWS_DEV * COLS_DEV, HEADS, HEAD_DIM)
        bias_win = bias_block.reshape(2 * ROWS_DEV, window_count, COLS_DEV, HEADS).transpose(1, 0, 2, 3).reshape(window_count, 2 * ROWS_DEV * COLS_DEV, HEADS)
        key_row = first_row - HALO + jnp.arange(2 * ROWS_DEV, dtype=jnp.int32)
        key_valid = jnp.repeat((key_row >= 0) & (key_row < GRID_R), COLS_DEV)
        scores = jnp.einsum('wqhd,wkhd->whqk', query_win.astype(jnp.float32), key_win.astype(jnp.float32)) * score_scale
        scores = scores + bias_win.astype(jnp.float32).transpose(0, 2, 1)[:, :, None, :]
        scores = jnp.where(key_valid[None, None, None, :], scores, -jnp.inf)
        top_score = lax.optimization_barrier(jnp.max(scores, axis=-1, keepdims=True))
        expo = jnp.exp(scores - top_score)
        weights = (expo / lax.optimization_barrier(jnp.sum(expo, axis=-1, keepdims=True))).astype(jnp.bfloat16)
        attended = jnp.einsum('whqk,wkhd->wqhd', weights.astype(jnp.float32), value_win.astype(jnp.float32)).astype(jnp.bfloat16)
        return attended.reshape(window_count, ROWS_DEV, COLS_DEV, D).transpose(1, 0, 2, 3).reshape(ROWS_DEV, GRID_C, D)
    attended = lax.map(window_block, jnp.arange(block_count, dtype=jnp.int32)).reshape(GRID_R * GRID_C, D)
    mixed = jnp.dot(attended, w_out, preferred_element_type=jnp.float32).reshape(GRID_R, GRID_C, D)
    return (lifted + mixed).astype(jnp.bfloat16)
```

```python
import functools

import jax
import jax.numpy as jnp
from jax import lax
from jax.experimental import pallas as pl
from jax.experimental.pallas import tpu as pltpu
from jax.sharding import PartitionSpec as P

ROWS_DEV = 8
COLS_DEV = 64
HALO = 4


def extended_2(cells, sides, width):
    for axis, dim in sides:
        count = lax.axis_size(axis)
        ends = count - 1
        head = lax.slice_in_dim(cells, 0, width, axis=dim)
        tail = lax.slice_in_dim(cells, cells.shape[dim] - width, cells.shape[dim], axis=dim)
        cells = jnp.concatenate(
            [
                lax.ppermute(tail, axis, [(i, (i + 1) % count) for i in range(ends)]),
                cells,
                lax.ppermute(head, axis, [((i + 1) % count, i) for i in range(ends)]),
            ],
            axis=dim,
        )
    return cells


def dense_body(
    image_tokens,
    lift_weight,
    route_token,
    route_cell,
    slot_counts,
    norm_gain,
    w_query,
    w_key,
    w_value,
    w_out,
    key_bias,
):
    tile_count = route_token.shape[2]
    slot_count = route_token.shape[3]
    width_out = lift_weight.shape[1]
    head_count = key_bias.shape[2]
    head_size = width_out // head_count
    grid_rows = key_bias.shape[0]
    own_cells = ROWS_DEV * COLS_DEV
    is_live = (
        lax.broadcasted_iota(jnp.int32, (tile_count, slot_count), 1) < slot_counts[0, 0][:, None]
    )
    token_index = route_token[0, 0]
    projected = jnp.dot(image_tokens, lift_weight, preferred_element_type=jnp.float32).astype(
        jnp.bfloat16
    )
    picked = jnp.where(is_live[:, :, None], projected[token_index], jnp.zeros((), jnp.bfloat16))
    arrived = lax.all_to_all(picked, ("bevy", "bevx"), split_axis=0, concat_axis=0, tiled=True)
    arrived_rows = arrived.reshape(tile_count * slot_count, -1)
    cell_index = route_cell[:, 0, 0, :].reshape(-1)
    both_rows, both_cells = (
        lax.all_gather(arrived_rows, "cam", axis=0, tiled=True),
        lax.all_gather(cell_index, "cam", axis=0, tiled=True),
    )
    first_cell = lax.axis_index("cam") * own_cells
    cell_ids = first_cell + lax.broadcasted_iota(jnp.int32, (own_cells, both_cells.shape[0]), 0)
    one_hot = (cell_ids == both_cells[None, :]).astype(jnp.bfloat16)
    lifted = jnp.dot(one_hot, both_rows, preferred_element_type=jnp.float32)
    mean_square = jnp.mean(lifted * lifted, axis=-1, keepdims=True)
    normed = (lifted * lax.rsqrt(mean_square + 1e-06) * norm_gain).astype(jnp.bfloat16)
    queries = jnp.dot(normed, w_query, preferred_element_type=jnp.float32).astype(jnp.bfloat16)
    row_start = lax.axis_index(("bevy", "cam")) * ROWS_DEV
    key_local = jnp.dot(normed, w_key, preferred_element_type=jnp.float32).astype(jnp.bfloat16)
    value_local = jnp.dot(normed, w_value, preferred_element_type=jnp.float32).astype(jnp.bfloat16)
    stacked = jnp.concatenate([key_local, value_local], axis=-1).reshape(
        ROWS_DEV, COLS_DEV, 2 * width_out
    )
    extended = extended_2(stacked, ((("bevy", "cam"), 0),), HALO).reshape(-1, 2 * width_out)
    key_vectors = extended[:, :width_out]
    value_vectors = extended[:, width_out:]
    bias_padded = jnp.pad(key_bias, ((HALO, HALO), (0, 0), (0, 0)))
    bias_rows = (
        lax.dynamic_slice_in_dim(bias_padded, row_start, 2 * ROWS_DEV, 0)
        .reshape(-1, head_count)
        .astype(jnp.float32)
    )
    key_row = row_start - HALO + jnp.arange(2 * ROWS_DEV, dtype=jnp.int32)
    key_valid = jnp.repeat((key_row >= 0) & (key_row < grid_rows), COLS_DEV)
    query_heads = queries.reshape(own_cells, head_count, head_size)
    key_heads = key_vectors.reshape(-1, head_count, head_size)
    value_heads = value_vectors.reshape(-1, head_count, head_size)
    score_scale = head_size ** (-0.5)
    scores = (
        jnp.einsum("qhd,khd->hqk", query_heads, key_heads, preferred_element_type=jnp.float32)
        * score_scale
    )
    scores = scores + bias_rows.T[:, None, :]
    scores = jnp.where(key_valid[None, None, :], scores, -jnp.inf)
    top_score = jnp.max(scores, axis=-1, keepdims=True)
    expo = jnp.exp(scores - top_score)
    weights = (expo / jnp.sum(expo, axis=-1, keepdims=True)).astype(jnp.bfloat16)
    attended = jnp.einsum(
        "hqk,khd->qhd", weights, value_heads, preferred_element_type=jnp.float32
    ).astype(jnp.bfloat16)
    attended = attended.reshape(own_cells, width_out)
    result = lifted + jnp.dot(attended, w_out, preferred_element_type=jnp.float32)
    return result.astype(jnp.bfloat16).reshape(ROWS_DEV, COLS_DEV, width_out)


COL_TILE = 256
NEVER = -1e30


def to_column(row):
    size = row.shape[1]
    across = lax.broadcasted_iota(jnp.int32, (size, size), 1)
    down = lax.broadcasted_iota(jnp.int32, (size, size), 0)
    return jnp.sum(jnp.where(across == down, row, 0), axis=1, keepdims=True)


def dot_last(left, right):
    return lax.dot_general(
        left, right, (((1,), (1,)), ((), ())), preferred_element_type=jnp.float32
    )


def slot_masks(cells, shift, exists, window):
    size = cells.shape[1]
    column = to_column(cells)
    same = column == cells
    down = lax.broadcasted_iota(jnp.int32, (size, size), 0)
    across = lax.broadcasted_iota(jnp.int32, (size, size), 1)
    repeat_row = jnp.sum(jnp.where(same & (down < across), 1, 0), axis=0, keepdims=True)
    repeat_col = jnp.sum(jnp.where(same & (across < down), 1, 0), axis=1, keepdims=True)

    def place(cell, repeat):
        spot = cell + shift
        keep = (repeat == 0) & (spot >= 0) & (spot < window) & exists
        return jnp.where(keep, spot, -1)

    return same.astype(jnp.bfloat16), place(cells, repeat_row), place(column, repeat_col)


def slot_attention(
    cam,
    row_start,
    grid_rows,
    cells_own,
    cells_side,
    rows_ref,
    bias_ref,
    gain_ref,
    lift_ref,
    query_w,
    key_w,
    value_w,
    out_w,
    out_ref,
    proj,
    lifted,
    normed,
    queries,
    keys,
    values,
    key_extra,
    rest_top,
    rest_sum,
    attended,
    wait_for,
):
    slots = cells_own.shape[1]
    heads, window = bias_ref.shape
    width = proj.shape[1]
    head_size = width // heads
    own_cells = ROWS_DEV * COLS_DEV
    tile_rows = 2 * ROWS_DEV
    halo_cells = HALO * COLS_DEV
    side_shift = (tile_rows - HALO) * COLS_DEV
    own_same, own_row, own_col = slot_masks(
        cells_own, halo_cells - cam * own_cells, True, window
    )
    side_exists = jnp.where(cam == 0, row_start > 0, row_start + ROWS_DEV < grid_rows)
    side_same, side_row, side_col = slot_masks(
        cells_side, jnp.where(cam == 0, -side_shift, side_shift), side_exists, window
    )
    spot_row = jnp.concatenate([own_row, side_row], axis=1)
    spot_col = jnp.concatenate([own_col, side_col], axis=0)
    hit = lax.broadcasted_iota(jnp.int32, (2 * slots, window), 1) == spot_col
    taken = jnp.max(jnp.where(hit, 1.0, 0.0), axis=0, keepdims=True) > 0.5
    bias = bias_ref[...]
    extra = dot_last(bias, hit.astype(jnp.bfloat16))
    extra = jnp.where(spot_row >= 0, extra, NEVER)
    key_extra[...] = extra
    window_row = row_start - HALO + lax.broadcasted_iota(jnp.int32, (1, window), 1) // COLS_DEV
    empty = jnp.logical_not(taken) & (window_row >= 0) & (window_row < grid_rows)
    rest = jnp.where(empty, bias.astype(jnp.float32), NEVER)
    top = jnp.max(rest, axis=1, keepdims=True)
    total = jnp.sum(jnp.where(empty, jnp.exp(rest - top), 0.0), axis=1, keepdims=True)
    rest_top[...] = jnp.broadcast_to(top, rest_top.shape)
    rest_sum[...] = jnp.broadcast_to(total, rest_sum.shape)

    wait_for("lift")

    @pl.loop(0, width // COL_TILE)
    def _(step):
        cols = pl.ds(pl.multiple_of(step * COL_TILE, COL_TILE), COL_TILE)
        proj[:, cols] = jnp.dot(
            rows_ref[...], lift_ref[:, cols], preferred_element_type=jnp.float32
        ).astype(jnp.bfloat16)
        lifted[:slots, cols] = jnp.dot(
            own_same, proj[:slots, cols], preferred_element_type=jnp.float32
        )
        lifted[slots:, cols] = jnp.dot(
            side_same, proj[slots:, cols], preferred_element_type=jnp.float32
        )

    whole = lifted[...]
    mean_square = jnp.mean(whole * whole, axis=-1, keepdims=True)
    normed[...] = (whole * lax.rsqrt(mean_square + 1e-06) * gain_ref[...]).astype(jnp.bfloat16)

    wait_for("qkv")

    @pl.loop(0, width // COL_TILE)
    def _(step):
        cols = pl.ds(pl.multiple_of(step * COL_TILE, COL_TILE), COL_TILE)
        made = jnp.dot(
            normed[:slots, :], query_w[:, cols], preferred_element_type=jnp.float32
        ).astype(jnp.bfloat16)
        queries[:, cols] = made * jnp.asarray(head_size**-0.5, jnp.bfloat16)
        keys[:, cols] = jnp.dot(
            normed[...], key_w[:, cols], preferred_element_type=jnp.float32
        ).astype(jnp.bfloat16)
        values[:, cols] = jnp.dot(
            normed[...], value_w[:, cols], preferred_element_type=jnp.float32
        ).astype(jnp.bfloat16)

    blank_top = jnp.maximum(jnp.max(extra, axis=1, keepdims=True), top)
    blank = jnp.exp(extra - blank_top)
    blank_sum = jnp.sum(blank, axis=1, keepdims=True) + total * jnp.exp(top - blank_top)
    blank = (blank / blank_sum).astype(jnp.bfloat16)
    blank = jnp.dot(blank, values[...], preferred_element_type=jnp.float32)
    lane_head = lax.broadcasted_iota(jnp.int32, (heads, width), 1) // head_size
    own_head = lax.broadcasted_iota(jnp.int32, (heads, width), 0) == lane_head
    blank = jnp.sum(jnp.where(own_head, blank, 0.0), axis=0, keepdims=True)
    attended[slots:, :] = jnp.broadcast_to(blank, (16, width)).astype(jnp.bfloat16)

    low = lax.broadcasted_iota(jnp.int32, (slots, 2 * head_size), 1) < head_size

    @pl.loop(0, heads // 4)
    def _(step):
        for inner in range(2):
            pair = step * 2 + inner
            cols = pl.ds(pl.multiple_of(pair * 2 * head_size, 2 * head_size), 2 * head_size)
            query = queries[:, cols]
            parts = []
            for side in range(2):
                head = pl.ds(pair * 2 + side, 1)
                mine = low if side == 0 else jnp.logical_not(low)
                score = dot_last(jnp.where(mine, query, jnp.zeros_like(query)), keys[:, cols])
                score = score + key_extra[head, :]
                rest_best = rest_top[head, :][:, :1]
                best = jnp.maximum(jnp.max(score, axis=1, keepdims=True), rest_best)
                expo = jnp.exp(score - best)
                weight_sum = jnp.sum(expo, axis=1, keepdims=True)
                weight_sum = weight_sum + rest_sum[head, :][:, :1] * jnp.exp(rest_best - best)
                mixed = jnp.dot(
                    expo.astype(jnp.bfloat16), values[:, cols], preferred_element_type=jnp.float32
                )
                parts.append(mixed / weight_sum)
            attended[:slots, cols] = jnp.where(low, parts[0], parts[1]).astype(jnp.bfloat16)

    cell = lax.broadcasted_iota(jnp.int32, (own_cells, slots), 0) + halo_cells
    spread = cell == own_row
    filled = jnp.max(jnp.where(spread, 1.0, 0.0), axis=1, keepdims=True) > 0.5
    spread = spread.astype(jnp.bfloat16)

    wait_for("out")

    @pl.loop(0, width // COL_TILE)
    def _(step):
        cols = pl.ds(pl.multiple_of(step * COL_TILE, COL_TILE), COL_TILE)
        mixed = jnp.dot(attended[...], out_w[:, cols], preferred_element_type=jnp.float32)
        final = (lifted[:slots, cols] + mixed[:slots]).astype(jnp.bfloat16)
        placed = jnp.dot(spread, final, preferred_element_type=jnp.float32)
        out_ref[:, cols] = jnp.where(filled, placed, mixed[slots : slots + 1]).astype(jnp.bfloat16)


def compute_scratch(slots, heads, width):
    return [
        pltpu.VMEM((2 * slots, width), jnp.bfloat16),
        pltpu.VMEM((2 * slots, width), jnp.float32),
        pltpu.VMEM((2 * slots, width), jnp.bfloat16),
        pltpu.VMEM((slots, width), jnp.bfloat16),
        pltpu.VMEM((2 * slots, width), jnp.bfloat16),
        pltpu.VMEM((2 * slots, width), jnp.bfloat16),
        pltpu.VMEM((heads, 2 * slots), jnp.float32),
        pltpu.VMEM((heads, 128), jnp.float32),
        pltpu.VMEM((heads, 128), jnp.float32),
        pltpu.VMEM((slots + 16, width), jnp.bfloat16),
    ]


def compute_kernel(
    grid_rows, cells_ref, rows_ref, bias_ref, gain_ref, lift_h, query_h, key_h, value_h, out_h,
    out_ref, lift_v, query_v, key_v, value_v, out_v, sems, *scratch
):
    pairs = [(lift_h, lift_v), (query_h, query_v), (key_h, key_v), (value_h, value_v), (out_h, out_v)]
    copies = [pltpu.make_async_copy(a, b, sems.at[i]) for i, (a, b) in enumerate(pairs)]
    for copy in copies:
        copy.start()

    def wait_for(name):
        for copy in {"lift": copies[:1], "qkv": copies[1:4], "out": copies[4:]}[name]:
            copy.wait()

    cam = lax.axis_index("cam")
    row_start = (lax.axis_index("bevy") * 2 + cam) * ROWS_DEV
    slot_attention(
        cam, row_start, grid_rows, cells_ref[0:1, :], cells_ref[1:2, :], rows_ref, bias_ref,
        gain_ref, lift_v, query_v, key_v, value_v, out_v, out_ref, *scratch, wait_for,
    )


def slot_body(
    image_tokens, lift_weight, route_token, route_cell, slot_counts, norm_gain, w_query, w_key,
    w_value, w_out, key_bias,
):
    tile_count, slot_count = route_token.shape[2:]
    width = lift_weight.shape[1]
    heads = key_bias.shape[2]
    grid_rows = key_bias.shape[0]
    live = lax.broadcasted_iota(jnp.int32, (tile_count, slot_count), 1) < slot_counts[0, 0][:, None]
    wanted = jnp.where(live, route_token[0, 0], -1).reshape(-1, 1)
    choose = (
        lax.broadcasted_iota(jnp.int32, (1, image_tokens.shape[0]), 1) == wanted
    ).astype(jnp.bfloat16)
    picked = jnp.dot(choose, image_tokens, preferred_element_type=jnp.float32).astype(jnp.bfloat16)
    picked = picked.reshape(tile_count, slot_count, -1)
    arrived = lax.all_to_all(picked, ("bevy", "bevx"), split_axis=0, concat_axis=0, tiled=True)
    arrived = arrived.reshape(tile_count * slot_count, -1)
    cells = route_cell[:, 0, 0, :].reshape(-1)
    swap = [(0, 1), (1, 0)]
    edge = 2 * lax.axis_size("bevy")
    across = [p for i in range(1, edge - 1, 2) for p in ((i, i + 1), (i + 1, i))]
    own_cells = jnp.concatenate([cells, lax.ppermute(cells, "cam", swap)])
    side_cells = lax.ppermute(own_cells, ("bevy", "cam"), across)
    own_rows = jnp.concatenate([arrived, lax.ppermute(arrived, "cam", swap)])
    side_rows = lax.ppermute(own_rows, ("bevy", "cam"), across)
    rows = jnp.concatenate([own_rows, side_rows])
    both_cells = jnp.stack([own_cells, side_cells])
    row_start = lax.axis_index(("bevy", "cam")) * ROWS_DEV
    padded = jnp.pad(key_bias, ((HALO, HALO), (0, 0), (0, 0)))
    window = lax.dynamic_slice_in_dim(padded, row_start, 2 * ROWS_DEV, 0)
    window = window.reshape(-1, heads).T
    slots = 2 * tile_count * slot_count
    vmem = pl.BlockSpec(memory_space=pltpu.VMEM)
    anywhere = pl.BlockSpec(memory_space=pl.ANY)
    weights = (lift_weight, w_query, w_key, w_value, w_out)
    out = pl.pallas_call(
        functools.partial(compute_kernel, grid_rows),
        out_shape=jax.ShapeDtypeStruct((ROWS_DEV * COLS_DEV, width), jnp.bfloat16),
        in_specs=[vmem] * 4 + [anywhere] * 5,
        out_specs=vmem,
        scratch_shapes=[pltpu.VMEM(w.shape, jnp.bfloat16) for w in weights]
        + [pltpu.SemaphoreType.DMA((5,))]
        + compute_scratch(slots, heads, width),
        compiler_params=pltpu.CompilerParams(vmem_limit_bytes=48 * 2**20),
    )(both_cells, rows, window, norm_gain.reshape(1, -1), *weights)
    return out.reshape(ROWS_DEV, COLS_DEV, width)


def solution(mesh):
    placed = (
        P(("bevy", "bevx", "cam"), None),
        P(),
        P(("bevy", "bevx"), "cam", None, None),
        P(None, "cam", ("bevy", "bevx"), None),
        P(("bevy", "bevx"), "cam", None),
        P(),
        P(),
        P(),
        P(),
        P(),
        P(None, "bevx", None),
    )
    tiles = mesh.shape["bevy"] * mesh.shape["bevx"]
    sparse = mesh.shape["cam"] == 2 and tiles <= 16
    return jax.shard_map(
        slot_body if sparse else dense_body,
        mesh=mesh,
        in_specs=placed,
        out_specs=P(("bevy", "cam"), "bevx", None),
        check_vma=False,
    )
```

```python
import functools

import jax
import jax.numpy as jnp
from jax import lax
from jax.experimental import pallas as pl
from jax.experimental.pallas import tpu as pltpu
from jax.sharding import PartitionSpec as P

ROWS_DEV = 8
COLS_DEV = 64
HALO = 4


def extended_2(cells, sides, width):
    for axis, dim in sides:
        count = lax.axis_size(axis)
        ends = count - 1
        head = lax.slice_in_dim(cells, 0, width, axis=dim)
        tail = lax.slice_in_dim(cells, cells.shape[dim] - width, cells.shape[dim], axis=dim)
        cells = jnp.concatenate(
            [
                lax.ppermute(tail, axis, [(i, (i + 1) % count) for i in range(ends)]),
                cells,
                lax.ppermute(head, axis, [((i + 1) % count, i) for i in range(ends)]),
            ],
            axis=dim,
        )
    return cells


def dense_body(
    image_tokens,
    lift_weight,
    route_token,
    route_cell,
    slot_counts,
    norm_gain,
    w_query,
    w_key,
    w_value,
    w_out,
    key_bias,
):
    tile_count = route_token.shape[2]
    slot_count = route_token.shape[3]
    width_out = lift_weight.shape[1]
    head_count = key_bias.shape[2]
    head_size = width_out // head_count
    grid_rows = key_bias.shape[0]
    own_cells = ROWS_DEV * COLS_DEV
    is_live = (
        lax.broadcasted_iota(jnp.int32, (tile_count, slot_count), 1) < slot_counts[0, 0][:, None]
    )
    token_index = route_token[0, 0]
    projected = jnp.dot(image_tokens, lift_weight, preferred_element_type=jnp.float32).astype(
        jnp.bfloat16
    )
    picked = jnp.where(is_live[:, :, None], projected[token_index], jnp.zeros((), jnp.bfloat16))
    arrived = lax.all_to_all(picked, ("bevy", "bevx"), split_axis=0, concat_axis=0, tiled=True)
    arrived_rows = arrived.reshape(tile_count * slot_count, -1)
    cell_index = route_cell[:, 0, 0, :].reshape(-1)
    both_rows, both_cells = (
        lax.all_gather(arrived_rows, "cam", axis=0, tiled=True),
        lax.all_gather(cell_index, "cam", axis=0, tiled=True),
    )
    first_cell = lax.axis_index("cam") * own_cells
    cell_ids = first_cell + lax.broadcasted_iota(jnp.int32, (own_cells, both_cells.shape[0]), 0)
    one_hot = (cell_ids == both_cells[None, :]).astype(jnp.bfloat16)
    lifted = jnp.dot(one_hot, both_rows, preferred_element_type=jnp.float32)
    mean_square = jnp.mean(lifted * lifted, axis=-1, keepdims=True)
    normed = (lifted * lax.rsqrt(mean_square + 1e-06) * norm_gain).astype(jnp.bfloat16)
    queries = jnp.dot(normed, w_query, preferred_element_type=jnp.float32).astype(jnp.bfloat16)
    row_start = lax.axis_index(("bevy", "cam")) * ROWS_DEV
    key_local = jnp.dot(normed, w_key, preferred_element_type=jnp.float32).astype(jnp.bfloat16)
    value_local = jnp.dot(normed, w_value, preferred_element_type=jnp.float32).astype(jnp.bfloat16)
    stacked = jnp.concatenate([key_local, value_local], axis=-1).reshape(
        ROWS_DEV, COLS_DEV, 2 * width_out
    )
    extended = extended_2(stacked, ((("bevy", "cam"), 0),), HALO).reshape(-1, 2 * width_out)
    key_vectors = extended[:, :width_out]
    value_vectors = extended[:, width_out:]
    bias_padded = jnp.pad(key_bias, ((HALO, HALO), (0, 0), (0, 0)))
    bias_rows = (
        lax.dynamic_slice_in_dim(bias_padded, row_start, 2 * ROWS_DEV, 0)
        .reshape(-1, head_count)
        .astype(jnp.float32)
    )
    key_row = row_start - HALO + jnp.arange(2 * ROWS_DEV, dtype=jnp.int32)
    key_valid = jnp.repeat((key_row >= 0) & (key_row < grid_rows), COLS_DEV)
    query_heads = queries.reshape(own_cells, head_count, head_size)
    key_heads = key_vectors.reshape(-1, head_count, head_size)
    value_heads = value_vectors.reshape(-1, head_count, head_size)
    score_scale = head_size ** (-0.5)
    scores = (
        jnp.einsum("qhd,khd->hqk", query_heads, key_heads, preferred_element_type=jnp.float32)
        * score_scale
    )
    scores = scores + bias_rows.T[:, None, :]
    scores = jnp.where(key_valid[None, None, :], scores, -jnp.inf)
    top_score = jnp.max(scores, axis=-1, keepdims=True)
    expo = jnp.exp(scores - top_score)
    weights = (expo / jnp.sum(expo, axis=-1, keepdims=True)).astype(jnp.bfloat16)
    attended = jnp.einsum(
        "hqk,khd->qhd", weights, value_heads, preferred_element_type=jnp.float32
    ).astype(jnp.bfloat16)
    attended = attended.reshape(own_cells, width_out)
    result = lifted + jnp.dot(attended, w_out, preferred_element_type=jnp.float32)
    return result.astype(jnp.bfloat16).reshape(ROWS_DEV, COLS_DEV, width_out)


COL_TILE = 256
NEVER = -1e30
SLOTS = 8


def to_column(row):
    size = row.shape[1]
    across = lax.broadcasted_iota(jnp.int32, (size, size), 1)
    down = lax.broadcasted_iota(jnp.int32, (size, size), 0)
    return jnp.sum(jnp.where(across == down, row, 0), axis=1, keepdims=True)


def dot_last(left, right):
    return lax.dot_general(
        left, right, (((1,), (1,)), ((), ())), preferred_element_type=jnp.float32
    )


def slot_masks(cells, shift, exists, window):
    size = cells.shape[1]
    column = to_column(cells)
    same = column == cells
    down = lax.broadcasted_iota(jnp.int32, (size, size), 0)
    across = lax.broadcasted_iota(jnp.int32, (size, size), 1)
    repeat_row = jnp.sum(jnp.where(same & (down < across), 1, 0), axis=0, keepdims=True)
    repeat_col = jnp.sum(jnp.where(same & (across < down), 1, 0), axis=1, keepdims=True)

    def place(cell, repeat):
        spot = cell + shift
        keep = (repeat == 0) & (spot >= 0) & (spot < window) & exists
        return jnp.where(keep, spot, -1)

    return same.astype(jnp.bfloat16), place(cells, repeat_row), place(column, repeat_col)


def slot_attention(
    cam,
    row_start,
    grid_rows,
    cells_own,
    cells_side,
    rows_ref,
    bias_ref,
    gain_ref,
    lift_ref,
    query_w,
    key_w,
    value_w,
    out_w,
    out_ref,
    lifted,
    normed,
    queries,
    keys,
    values,
    key_extra,
    rest_top,
    rest_sum,
    attended,
    wait_for,
):
    slots = cells_own.shape[1]
    heads, window = bias_ref.shape
    width = lifted.shape[1]
    head_size = width // heads
    own_cells = ROWS_DEV * COLS_DEV
    tile_rows = 2 * ROWS_DEV
    halo_cells = HALO * COLS_DEV
    side_shift = (tile_rows - HALO) * COLS_DEV
    own_same, own_row, own_col = slot_masks(
        cells_own, halo_cells - cam * own_cells, True, window
    )
    side_exists = jnp.where(cam == 0, row_start > 0, row_start + ROWS_DEV < grid_rows)
    side_same, side_row, side_col = slot_masks(
        cells_side, jnp.where(cam == 0, -side_shift, side_shift), side_exists, window
    )
    spot_row = jnp.concatenate([own_row, side_row], axis=1)
    spot_col = jnp.concatenate([own_col, side_col], axis=0)
    hit = lax.broadcasted_iota(jnp.int32, (2 * slots, window), 1) == spot_col
    taken = jnp.max(jnp.where(hit, 1.0, 0.0), axis=0, keepdims=True) > 0.5
    bias = bias_ref[...]
    extra = dot_last(bias, hit.astype(jnp.bfloat16))
    extra = jnp.where(spot_row >= 0, extra, NEVER)
    key_extra[...] = extra
    window_row = row_start - HALO + lax.broadcasted_iota(jnp.int32, (1, window), 1) // COLS_DEV
    empty = jnp.logical_not(taken) & (window_row >= 0) & (window_row < grid_rows)
    rest = jnp.where(empty, bias.astype(jnp.float32), NEVER)
    top = jnp.max(rest, axis=1, keepdims=True)
    total = jnp.sum(jnp.where(empty, jnp.exp(rest - top), 0.0), axis=1, keepdims=True)
    rest_top[...] = jnp.broadcast_to(top, rest_top.shape)
    rest_sum[...] = jnp.broadcast_to(total, rest_sum.shape)

    def lift_group(group, same):
        part = pl.ds(group * slots, slots)

        @pl.loop(0, width // COL_TILE)
        def _(step):
            cols = pl.ds(pl.multiple_of(step * COL_TILE, COL_TILE), COL_TILE)
            made = jnp.dot(rows_ref[part, :], lift_ref[:, cols], preferred_element_type=jnp.float32)
            lifted[part, cols] = jnp.dot(
                same, made.astype(jnp.bfloat16), preferred_element_type=jnp.float32
            )

        whole = lifted[part, :]
        mean_square = jnp.mean(whole * whole, axis=-1, keepdims=True)
        normed[part, :] = (whole * lax.rsqrt(mean_square + 1e-06) * gain_ref[...]).astype(
            jnp.bfloat16
        )

    def key_group(group):
        part = pl.ds(group * slots, slots)

        @pl.loop(0, width // COL_TILE)
        def _(step):
            cols = pl.ds(pl.multiple_of(step * COL_TILE, COL_TILE), COL_TILE)
            if group == 0:
                made = jnp.dot(
                    normed[part, :], query_w[:, cols], preferred_element_type=jnp.float32
                ).astype(jnp.bfloat16)
                queries[:, cols] = made * jnp.asarray(head_size**-0.5, jnp.bfloat16)
            keys[part, cols] = jnp.dot(
                normed[part, :], key_w[:, cols], preferred_element_type=jnp.float32
            ).astype(jnp.bfloat16)
            values[part, cols] = jnp.dot(
                normed[part, :], value_w[:, cols], preferred_element_type=jnp.float32
            ).astype(jnp.bfloat16)

    wait_for("own")
    wait_for("lift")
    lift_group(0, own_same)
    wait_for("qkv")
    key_group(0)
    wait_for("side")
    lift_group(1, side_same)
    key_group(1)

    blank_top = jnp.maximum(jnp.max(extra, axis=1, keepdims=True), top)
    blank = jnp.exp(extra - blank_top)
    blank_sum = jnp.sum(blank, axis=1, keepdims=True) + total * jnp.exp(top - blank_top)
    blank = (blank / blank_sum).astype(jnp.bfloat16)
    blank = jnp.dot(blank, values[...], preferred_element_type=jnp.float32)
    lane_head = lax.broadcasted_iota(jnp.int32, (heads, width), 1) // head_size
    own_head = lax.broadcasted_iota(jnp.int32, (heads, width), 0) == lane_head
    blank = jnp.sum(jnp.where(own_head, blank, 0.0), axis=0, keepdims=True)
    attended[slots:, :] = jnp.broadcast_to(blank, (16, width)).astype(jnp.bfloat16)

    low = lax.broadcasted_iota(jnp.int32, (slots, 2 * head_size), 1) < head_size

    @pl.loop(0, heads // 4)
    def _(step):
        for inner in range(2):
            pair = step * 2 + inner
            cols = pl.ds(pl.multiple_of(pair * 2 * head_size, 2 * head_size), 2 * head_size)
            query = queries[:, cols]
            parts = []
            for side in range(2):
                head = pl.ds(pair * 2 + side, 1)
                mine = low if side == 0 else jnp.logical_not(low)
                score = dot_last(jnp.where(mine, query, jnp.zeros_like(query)), keys[:, cols])
                score = score + key_extra[head, :]
                rest_best = rest_top[head, :][:, :1]
                best = jnp.maximum(jnp.max(score, axis=1, keepdims=True), rest_best)
                expo = jnp.exp(score - best)
                weight_sum = jnp.sum(expo, axis=1, keepdims=True)
                weight_sum = weight_sum + rest_sum[head, :][:, :1] * jnp.exp(rest_best - best)
                mixed = jnp.dot(
                    expo.astype(jnp.bfloat16), values[:, cols], preferred_element_type=jnp.float32
                )
                parts.append(mixed / weight_sum)
            attended[:slots, cols] = jnp.where(low, parts[0], parts[1]).astype(jnp.bfloat16)

    cell = lax.broadcasted_iota(jnp.int32, (own_cells, slots), 0) + halo_cells
    spread = cell == own_row
    filled = jnp.max(jnp.where(spread, 1.0, 0.0), axis=1, keepdims=True) > 0.5
    spread = spread.astype(jnp.bfloat16)

    wait_for("out")

    @pl.loop(0, width // COL_TILE)
    def _(step):
        cols = pl.ds(pl.multiple_of(step * COL_TILE, COL_TILE), COL_TILE)
        mixed = jnp.dot(attended[...], out_w[:, cols], preferred_element_type=jnp.float32)
        final = (lifted[:slots, cols] + mixed[:slots]).astype(jnp.bfloat16)
        placed = jnp.dot(spread, final, preferred_element_type=jnp.float32)
        out_ref[:, cols] = jnp.where(filled, placed, mixed[slots : slots + 1]).astype(jnp.bfloat16)


def compute_scratch(slots, heads, width):
    return [
        pltpu.VMEM((2 * slots, width), jnp.float32),
        pltpu.VMEM((2 * slots, width), jnp.bfloat16),
        pltpu.VMEM((slots, width), jnp.bfloat16),
        pltpu.VMEM((2 * slots, width), jnp.bfloat16),
        pltpu.VMEM((2 * slots, width), jnp.bfloat16),
        pltpu.VMEM((heads, 2 * slots), jnp.float32),
        pltpu.VMEM((heads, 128), jnp.float32),
        pltpu.VMEM((heads, 128), jnp.float32),
        pltpu.VMEM((slots + 16, width), jnp.bfloat16),
    ]


def fused_kernel(
    grid_rows, wanted_ref, cells_ref, tokens_ref, bias_ref, gain_ref, lift_h, query_h, key_h,
    value_h, out_h, out_ref, lift_v, query_v, key_v, value_v, out_v, weight_sems, sent, landed,
    cells, rows, local_sem, tile_send, tile_recv, core_send, core_recv, side_send, side_recv,
    cell_send, cell_recv, *scratch
):
    bevy, bevx, cam = (lax.axis_index(name) for name in ("bevy", "bevx", "cam"))
    count_y, count_x = lax.axis_size("bevy"), lax.axis_size("bevx")
    tiles = count_y * count_x
    me = bevy * count_x + bevx
    block = 2 * SLOTS
    group = count_x * block
    half = sent.shape[1]
    mesh_id = pl.DeviceIdType.MESH
    has_up = bevy > 0
    has_down = bevy < count_y - 1
    has_side = jnp.where(cam == 0, bevy, count_y - 1 - bevy) > 0
    mate = (bevy, bevx, 1 - cam)
    up = (bevy - 1, bevx, 1)
    down = (bevy + 1, bevx, 0)
    across = (bevy + 2 * cam - 1, bevx, 1 - cam)

    barrier = pltpu.get_barrier_semaphore()

    @pl.loop(1, tiles)
    def _(step):
        peer = (me + step) % tiles
        pl.semaphore_signal(
            barrier, inc=1, device_id=(peer // count_x, peer % count_x, cam), device_id_type=mesh_id
        )

    pl.semaphore_signal(barrier, inc=1, device_id=mate, device_id_type=mesh_id)

    @pl.when(has_side)
    def _():
        pl.semaphore_signal(barrier, inc=1, device_id=across, device_id_type=mesh_id)

    wanted = to_column(wanted_ref[...])
    choose = lax.broadcasted_iota(jnp.int32, (wanted.shape[0], tokens_ref.shape[0]), 1) == wanted
    choose = choose.astype(jnp.bfloat16)
    left = jnp.dot(choose, tokens_ref[:, :half], preferred_element_type=jnp.float32)
    right = jnp.dot(choose, tokens_ref[:, half:], preferred_element_type=jnp.float32)
    in_block = lax.broadcasted_iota(jnp.int32, left.shape, 0) % block
    sent[...] = jnp.where(in_block < SLOTS, left, right).astype(jnp.bfloat16)

    pl.semaphore_wait(barrier, tiles + jnp.where(has_side, 1, 0))

    def at(start, size):
        return pl.ds(pl.multiple_of(start, block), size)

    def tile_copy(peer, slot):
        return pltpu.make_async_remote_copy(
            src_ref=sent.at[at(peer * block, block)],
            dst_ref=landed.at[cam, at(slot * block, block)],
            send_sem=tile_send.at[peer],
            recv_sem=tile_recv.at[slot],
            device_id=(peer // count_x, peer % count_x, cam),
            device_id_type=mesh_id,
        )

    @pl.loop(1, tiles)
    def _(step):
        tile_copy((me + step) % tiles, me).start()

    kept = pltpu.make_async_copy(
        sent.at[at(me * block, block)], landed.at[cam, at(me * block, block)], local_sem.at[0]
    )
    kept.start()
    own_cells = pltpu.make_async_copy(cells_ref, cells.at[cam], local_sem.at[1])
    own_cells.start()

    def cell_copy(target, slot, index, source):
        return pltpu.make_async_remote_copy(
            src_ref=cells_ref,
            dst_ref=cells.at[slot],
            send_sem=cell_send.at[index],
            recv_sem=cell_recv.at[slot],
            device_id=target,
            device_id_type=mesh_id,
        )

    def row_copy(target, slot, part, send, recv):
        return pltpu.make_async_remote_copy(
            src_ref=landed.at[cam, at(part * group, group)],
            dst_ref=landed.at[slot, at(part * group, group)],
            send_sem=send,
            recv_sem=recv,
            device_id=target,
            device_id_type=mesh_id,
        )

    def mate_rows(part, slot):
        return row_copy(mate, slot, part, core_send.at[part], core_recv.at[part])

    def side_rows(target, which, part, source):
        return row_copy(
            target, 2 + source, part, side_send.at[which, part], side_recv.at[source, part]
        )

    cell_copy(mate, cam, 0, cam).start()

    @pl.when(has_up)
    def _():
        cell_copy(up, 2 + cam, 1, cam).start()

    @pl.when(has_down)
    def _():
        cell_copy(down, 2 + cam, 2, cam).start()

    pairs = [(lift_h, lift_v), (query_h, query_v), (key_h, key_v), (value_h, value_v), (out_h, out_v)]
    copies = [pltpu.make_async_copy(a, b, weight_sems.at[i]) for i, (a, b) in enumerate(pairs)]
    for copy in copies:
        copy.start()

    kept.wait()

    @pl.loop(0, count_y)
    def _(step):
        part = (bevy + step) % count_y

        @pl.loop(0, count_x)
        def _(index):
            source = part * count_x + index

            @pl.when(source != me)
            def _():
                tile_copy(source, source).wait_recv()

        mate_rows(part, cam).start()

        @pl.when(has_up)
        def _():
            side_rows(up, 0, part, cam).start()

        @pl.when(has_down)
        def _():
            side_rows(down, 1, part, cam).start()

    own_cells.wait()
    cell_copy(mate, 1 - cam, 0, cam).wait_recv()

    @pl.when(has_side)
    def _():
        cell_copy(across, 2, 0, cam).wait_recv()
        cell_copy(across, 3, 0, cam).wait_recv()

    @pl.when(jnp.logical_not(has_side))
    def _():
        cells[2:] = jnp.zeros_like(cells[2:])
        landed[2:] = jnp.zeros_like(landed[2:])

    slots = rows.shape[0] // 4

    def join_halves(index):
        slot = lax.broadcasted_iota(jnp.int32, (slots, landed.shape[1]), 0)
        row = lax.broadcasted_iota(jnp.int32, (slots, landed.shape[1]), 1)
        first = slot // SLOTS * block + slot % SLOTS
        for side in range(2):
            take = (row == first + side * SLOTS).astype(jnp.bfloat16)
            rows[index * slots : (index + 1) * slots, side * half : (side + 1) * half] = jnp.dot(
                take, landed[index], preferred_element_type=jnp.float32
            ).astype(jnp.bfloat16)

    def wait_for(name):
        if name == "own":

            @pl.loop(0, count_y)
            def _(part):
                mate_rows(part, 1 - cam).wait_recv()

            join_halves(0)
            join_halves(1)
            return
        if name == "side":

            @pl.when(has_side)
            def _():
                @pl.loop(0, count_y)
                def _(part):
                    side_rows(across, 0, part, 0).wait_recv()
                    side_rows(across, 0, part, 1).wait_recv()

            join_halves(2)
            join_halves(3)
            return
        for copy in {"lift": copies[:1], "qkv": copies[1:4], "out": copies[4:]}[name]:
            copy.wait()

    row_start = (bevy * 2 + cam) * ROWS_DEV
    cells_own = jnp.concatenate([cells[0, 0:1, :], cells[1, 0:1, :]], axis=1)
    cells_side = jnp.concatenate([cells[2, 0:1, :], cells[3, 0:1, :]], axis=1)
    slot_attention(
        cam, row_start, grid_rows, cells_own, cells_side, rows, bias_ref, gain_ref, lift_v, query_v,
        key_v, value_v, out_v, out_ref, *scratch, wait_for,
    )

    @pl.loop(1, tiles)
    def _(step):
        tile_copy((me + step) % tiles, me).wait_send()

    @pl.loop(0, count_y)
    def _(part):
        mate_rows(part, cam).wait_send()

    cell_copy(mate, cam, 0, cam).wait_send()

    @pl.when(has_up)
    def _():
        cell_copy(up, 2 + cam, 1, cam).wait_send()

        @pl.loop(0, count_y)
        def _(part):
            side_rows(up, 0, part, cam).wait_send()

    @pl.when(has_down)
    def _():
        cell_copy(down, 2 + cam, 2, cam).wait_send()

        @pl.loop(0, count_y)
        def _(part):
            side_rows(down, 1, part, cam).wait_send()


def slot_body(
    image_tokens, lift_weight, route_token, route_cell, slot_counts, norm_gain, w_query, w_key,
    w_value, w_out, key_bias,
):
    tile_count, slot_count = route_token.shape[2:]
    width = lift_weight.shape[1]
    heads = key_bias.shape[2]
    grid_rows = key_bias.shape[0]
    half = image_tokens.shape[1] // 2
    live = lax.broadcasted_iota(jnp.int32, (tile_count, slot_count), 1) < slot_counts[0, 0][:, None]
    wanted = jnp.where(live, route_token[0, 0], -1)[:, None, :]
    wanted = jnp.broadcast_to(wanted, (tile_count, 2, slot_count)).reshape(1, -1)
    cells = jnp.broadcast_to(route_cell.reshape(1, -1), (8, tile_count * slot_count))
    row_start = lax.axis_index(("bevy", "cam")) * ROWS_DEV
    padded = jnp.pad(key_bias, ((HALO, HALO), (0, 0), (0, 0)))
    window = lax.dynamic_slice_in_dim(padded, row_start, 2 * ROWS_DEV, 0)
    window = window.reshape(-1, heads).T
    slots = 2 * tile_count * slot_count
    vmem = pl.BlockSpec(memory_space=pltpu.VMEM)
    anywhere = pl.BlockSpec(memory_space=pl.ANY)
    weights = (lift_weight, w_query, w_key, w_value, w_out)
    count_y = lax.axis_size("bevy")
    dma = pltpu.SemaphoreType.DMA
    out = pl.pallas_call(
        functools.partial(fused_kernel, grid_rows),
        out_shape=jax.ShapeDtypeStruct((ROWS_DEV * COLS_DEV, width), jnp.bfloat16),
        in_specs=[vmem] * 5 + [anywhere] * 5,
        out_specs=vmem,
        scratch_shapes=[pltpu.VMEM(w.shape, jnp.bfloat16) for w in weights]
        + [
            dma((5,)),
            pltpu.VMEM((slots, half), jnp.bfloat16),
            pltpu.VMEM((4, slots, half), jnp.bfloat16),
            pltpu.VMEM((4,) + cells.shape, jnp.int32),
            pltpu.VMEM((2 * slots, 2 * half), jnp.bfloat16),
            dma((2,)),
            dma((tile_count,)),
            dma((tile_count,)),
            dma((count_y,)),
            dma((count_y,)),
            dma((2, count_y)),
            dma((2, count_y)),
            dma((3,)),
            dma((4,)),
        ]
        + compute_scratch(slots, heads, width),
        compiler_params=pltpu.CompilerParams(
            vmem_limit_bytes=48 * 2**20, collective_id=0, has_side_effects=True
        ),
    )(wanted, cells, image_tokens, window, norm_gain.reshape(1, -1), *weights)
    return out.reshape(ROWS_DEV, COLS_DEV, width)


def solution(mesh):
    placed = (
        P(("bevy", "bevx", "cam"), None),
        P(),
        P(("bevy", "bevx"), "cam", None, None),
        P(None, "cam", ("bevy", "bevx"), None),
        P(("bevy", "bevx"), "cam", None),
        P(),
        P(),
        P(),
        P(),
        P(),
        P(None, "bevx", None),
    )
    tiles = mesh.shape["bevy"] * mesh.shape["bevx"]
    sparse = mesh.shape["cam"] == 2 and tiles <= 16
    return jax.shard_map(
        slot_body if sparse else dense_body,
        mesh=mesh,
        in_specs=placed,
        out_specs=P(("bevy", "cam"), "bevx", None),
        check_vma=False,
    )
```

```python
import functools

import jax
import jax.numpy as jnp
from jax import lax
from jax.experimental import pallas as pl
from jax.experimental.pallas import tpu as pltpu
from jax.sharding import PartitionSpec as P

ROWS_DEV = 8
COLS_DEV = 64
HALO = 4


def extended_2(cells, sides, width):
    for axis, dim in sides:
        count = lax.axis_size(axis)
        ends = count - 1
        head = lax.slice_in_dim(cells, 0, width, axis=dim)
        tail = lax.slice_in_dim(cells, cells.shape[dim] - width, cells.shape[dim], axis=dim)
        cells = jnp.concatenate(
            [
                lax.ppermute(tail, axis, [(i, (i + 1) % count) for i in range(ends)]),
                cells,
                lax.ppermute(head, axis, [((i + 1) % count, i) for i in range(ends)]),
            ],
            axis=dim,
        )
    return cells


def dense_body(
    image_tokens,
    lift_weight,
    route_token,
    route_cell,
    slot_counts,
    norm_gain,
    w_query,
    w_key,
    w_value,
    w_out,
    key_bias,
):
    tile_count = route_token.shape[2]
    slot_count = route_token.shape[3]
    width_out = lift_weight.shape[1]
    head_count = key_bias.shape[2]
    head_size = width_out // head_count
    grid_rows = key_bias.shape[0]
    own_cells = ROWS_DEV * COLS_DEV
    is_live = (
        lax.broadcasted_iota(jnp.int32, (tile_count, slot_count), 1) < slot_counts[0, 0][:, None]
    )
    token_index = route_token[0, 0]
    projected = jnp.dot(image_tokens, lift_weight, preferred_element_type=jnp.float32).astype(
        jnp.bfloat16
    )
    picked = jnp.where(is_live[:, :, None], projected[token_index], jnp.zeros((), jnp.bfloat16))
    arrived = lax.all_to_all(picked, ("bevy", "bevx"), split_axis=0, concat_axis=0, tiled=True)
    arrived_rows = arrived.reshape(tile_count * slot_count, -1)
    cell_index = route_cell[:, 0, 0, :].reshape(-1)
    both_rows, both_cells = (
        lax.all_gather(arrived_rows, "cam", axis=0, tiled=True),
        lax.all_gather(cell_index, "cam", axis=0, tiled=True),
    )
    first_cell = lax.axis_index("cam") * own_cells
    cell_ids = first_cell + lax.broadcasted_iota(jnp.int32, (own_cells, both_cells.shape[0]), 0)
    one_hot = (cell_ids == both_cells[None, :]).astype(jnp.bfloat16)
    lifted = jnp.dot(one_hot, both_rows, preferred_element_type=jnp.float32)
    mean_square = jnp.mean(lifted * lifted, axis=-1, keepdims=True)
    normed = (lifted * lax.rsqrt(mean_square + 1e-06) * norm_gain).astype(jnp.bfloat16)
    queries = jnp.dot(normed, w_query, preferred_element_type=jnp.float32).astype(jnp.bfloat16)
    row_start = lax.axis_index(("bevy", "cam")) * ROWS_DEV
    key_local = jnp.dot(normed, w_key, preferred_element_type=jnp.float32).astype(jnp.bfloat16)
    value_local = jnp.dot(normed, w_value, preferred_element_type=jnp.float32).astype(jnp.bfloat16)
    stacked = jnp.concatenate([key_local, value_local], axis=-1).reshape(
        ROWS_DEV, COLS_DEV, 2 * width_out
    )
    extended = extended_2(stacked, ((("bevy", "cam"), 0),), HALO).reshape(-1, 2 * width_out)
    key_vectors = extended[:, :width_out]
    value_vectors = extended[:, width_out:]
    bias_padded = jnp.pad(key_bias, ((HALO, HALO), (0, 0), (0, 0)))
    bias_rows = (
        lax.dynamic_slice_in_dim(bias_padded, row_start, 2 * ROWS_DEV, 0)
        .reshape(-1, head_count)
        .astype(jnp.float32)
    )
    key_row = row_start - HALO + jnp.arange(2 * ROWS_DEV, dtype=jnp.int32)
    key_valid = jnp.repeat((key_row >= 0) & (key_row < grid_rows), COLS_DEV)
    query_heads = queries.reshape(own_cells, head_count, head_size)
    key_heads = key_vectors.reshape(-1, head_count, head_size)
    value_heads = value_vectors.reshape(-1, head_count, head_size)
    score_scale = head_size ** (-0.5)
    scores = (
        jnp.einsum("qhd,khd->hqk", query_heads, key_heads, preferred_element_type=jnp.float32)
        * score_scale
    )
    scores = scores + bias_rows.T[:, None, :]
    scores = jnp.where(key_valid[None, None, :], scores, -jnp.inf)
    top_score = jnp.max(scores, axis=-1, keepdims=True)
    expo = jnp.exp(scores - top_score)
    weights = (expo / jnp.sum(expo, axis=-1, keepdims=True)).astype(jnp.bfloat16)
    attended = jnp.einsum(
        "hqk,khd->qhd", weights, value_heads, preferred_element_type=jnp.float32
    ).astype(jnp.bfloat16)
    attended = attended.reshape(own_cells, width_out)
    result = lifted + jnp.dot(attended, w_out, preferred_element_type=jnp.float32)
    return result.astype(jnp.bfloat16).reshape(ROWS_DEV, COLS_DEV, width_out)


COL_TILE = 256
NEVER = -1e30
SLOTS = 8


def to_column(row):
    size = row.shape[1]
    across = lax.broadcasted_iota(jnp.int32, (size, size), 1)
    down = lax.broadcasted_iota(jnp.int32, (size, size), 0)
    return jnp.sum(jnp.where(across == down, row, 0), axis=1, keepdims=True)


def dot_last(left, right):
    return lax.dot_general(
        left, right, (((1,), (1,)), ((), ())), preferred_element_type=jnp.float32
    )


def slot_masks(cells, shift, exists, window):
    size = cells.shape[1]
    column = to_column(cells)
    same = column == cells
    down = lax.broadcasted_iota(jnp.int32, (size, size), 0)
    across = lax.broadcasted_iota(jnp.int32, (size, size), 1)
    repeat_row = jnp.sum(jnp.where(same & (down < across), 1, 0), axis=0, keepdims=True)
    repeat_col = jnp.sum(jnp.where(same & (across < down), 1, 0), axis=1, keepdims=True)

    def place(cell, repeat):
        spot = cell + shift
        keep = (repeat == 0) & (spot >= 0) & (spot < window) & exists
        return jnp.where(keep, spot, -1)

    return same.astype(jnp.bfloat16), place(cells, repeat_row), place(column, repeat_col)


def slot_attention(
    cam,
    row_start,
    grid_rows,
    cells_own,
    cells_side,
    rows_ref,
    bias_ref,
    gain_ref,
    lift_ref,
    query_w,
    key_w,
    value_w,
    out_w,
    out_ref,
    lifted,
    normed,
    queries,
    keys,
    values,
    key_extra,
    rest_top,
    rest_sum,
    attended,
    wait_for,
):
    slots = cells_own.shape[1]
    heads, window = bias_ref.shape
    width = lifted.shape[1]
    head_size = width // heads
    own_cells = ROWS_DEV * COLS_DEV
    tile_rows = 2 * ROWS_DEV
    halo_cells = HALO * COLS_DEV
    side_shift = (tile_rows - HALO) * COLS_DEV
    own_same, own_row, own_col = slot_masks(
        cells_own, halo_cells - cam * own_cells, True, window
    )
    side_exists = jnp.where(cam == 0, row_start > 0, row_start + ROWS_DEV < grid_rows)
    side_same, side_row, side_col = slot_masks(
        cells_side, jnp.where(cam == 0, -side_shift, side_shift), side_exists, window
    )
    spot_row = jnp.concatenate([own_row, side_row], axis=1)
    spot_col = jnp.concatenate([own_col, side_col], axis=0)
    hit = lax.broadcasted_iota(jnp.int32, (2 * slots, window), 1) == spot_col
    taken = jnp.max(jnp.where(hit, 1.0, 0.0), axis=0, keepdims=True) > 0.5
    bias = bias_ref[...]
    extra = dot_last(bias, hit.astype(jnp.bfloat16))
    extra = jnp.where(spot_row >= 0, extra, NEVER)
    key_extra[...] = extra
    window_row = row_start - HALO + lax.broadcasted_iota(jnp.int32, (1, window), 1) // COLS_DEV
    empty = jnp.logical_not(taken) & (window_row >= 0) & (window_row < grid_rows)
    rest = jnp.where(empty, bias.astype(jnp.float32), NEVER)
    top = jnp.max(rest, axis=1, keepdims=True)
    total = jnp.sum(jnp.where(empty, jnp.exp(rest - top), 0.0), axis=1, keepdims=True)
    rest_top[...] = jnp.broadcast_to(top, rest_top.shape)
    rest_sum[...] = jnp.broadcast_to(total, rest_sum.shape)

    def lift_group(group, same):
        part = pl.ds(group * slots, slots)

        @pl.loop(0, width // COL_TILE)
        def _(step):
            cols = pl.ds(pl.multiple_of(step * COL_TILE, COL_TILE), COL_TILE)
            made = jnp.dot(rows_ref[part, :], lift_ref[:, cols], preferred_element_type=jnp.float32)
            lifted[part, cols] = jnp.dot(
                same, made.astype(jnp.bfloat16), preferred_element_type=jnp.float32
            )

        whole = lifted[part, :]
        mean_square = jnp.mean(whole * whole, axis=-1, keepdims=True)
        normed[part, :] = (whole * lax.rsqrt(mean_square + 1e-06) * gain_ref[...]).astype(
            jnp.bfloat16
        )

    def key_group(group):
        part = pl.ds(group * slots, slots)

        @pl.loop(0, width // COL_TILE)
        def _(step):
            cols = pl.ds(pl.multiple_of(step * COL_TILE, COL_TILE), COL_TILE)
            if group == 0:
                made = jnp.dot(
                    normed[part, :], query_w[:, cols], preferred_element_type=jnp.float32
                ).astype(jnp.bfloat16)
                queries[:, cols] = made * jnp.asarray(head_size**-0.5, jnp.bfloat16)
            keys[part, cols] = jnp.dot(
                normed[part, :], key_w[:, cols], preferred_element_type=jnp.float32
            ).astype(jnp.bfloat16)
            values[part, cols] = jnp.dot(
                normed[part, :], value_w[:, cols], preferred_element_type=jnp.float32
            ).astype(jnp.bfloat16)

    wait_for("own")
    wait_for("lift")
    lift_group(0, own_same)
    wait_for("qkv")
    key_group(0)
    wait_for("side")
    lift_group(1, side_same)
    key_group(1)

    blank_top = jnp.maximum(jnp.max(extra, axis=1, keepdims=True), top)
    blank = jnp.exp(extra - blank_top)
    blank_sum = jnp.sum(blank, axis=1, keepdims=True) + total * jnp.exp(top - blank_top)
    blank = (blank / blank_sum).astype(jnp.bfloat16)
    blank = jnp.dot(blank, values[...], preferred_element_type=jnp.float32)
    lane_head = lax.broadcasted_iota(jnp.int32, (heads, width), 1) // head_size
    own_head = lax.broadcasted_iota(jnp.int32, (heads, width), 0) == lane_head
    blank = jnp.sum(jnp.where(own_head, blank, 0.0), axis=0, keepdims=True)
    attended[slots:, :] = jnp.broadcast_to(blank, (16, width)).astype(jnp.bfloat16)

    low = lax.broadcasted_iota(jnp.int32, (slots, 2 * head_size), 1) < head_size

    @pl.loop(0, heads // 4)
    def _(step):
        for inner in range(2):
            pair = step * 2 + inner
            cols = pl.ds(pl.multiple_of(pair * 2 * head_size, 2 * head_size), 2 * head_size)
            query = queries[:, cols]
            parts = []
            for side in range(2):
                head = pl.ds(pair * 2 + side, 1)
                mine = low if side == 0 else jnp.logical_not(low)
                score = dot_last(jnp.where(mine, query, jnp.zeros_like(query)), keys[:, cols])
                score = score + key_extra[head, :]
                rest_best = rest_top[head, :][:, :1]
                best = jnp.maximum(jnp.max(score, axis=1, keepdims=True), rest_best)
                expo = jnp.exp(score - best)
                weight_sum = jnp.sum(expo, axis=1, keepdims=True)
                weight_sum = weight_sum + rest_sum[head, :][:, :1] * jnp.exp(rest_best - best)
                mixed = jnp.dot(
                    expo.astype(jnp.bfloat16), values[:, cols], preferred_element_type=jnp.float32
                )
                parts.append(mixed / weight_sum)
            attended[:slots, cols] = jnp.where(low, parts[0], parts[1]).astype(jnp.bfloat16)

    cell = lax.broadcasted_iota(jnp.int32, (own_cells, slots), 0) + halo_cells
    spread = cell == own_row
    filled = jnp.max(jnp.where(spread, 1.0, 0.0), axis=1, keepdims=True) > 0.5
    spread = spread.astype(jnp.bfloat16)

    wait_for("out")

    @pl.loop(0, width // COL_TILE)
    def _(step):
        cols = pl.ds(pl.multiple_of(step * COL_TILE, COL_TILE), COL_TILE)
        mixed = jnp.dot(attended[...], out_w[:, cols], preferred_element_type=jnp.float32)
        final = (lifted[:slots, cols] + mixed[:slots]).astype(jnp.bfloat16)
        placed = jnp.dot(spread, final, preferred_element_type=jnp.float32)
        out_ref[:, cols] = jnp.where(filled, placed, mixed[slots : slots + 1]).astype(jnp.bfloat16)


def compute_scratch(slots, heads, width):
    return [
        pltpu.VMEM((2 * slots, width), jnp.float32),
        pltpu.VMEM((2 * slots, width), jnp.bfloat16),
        pltpu.VMEM((slots, width), jnp.bfloat16),
        pltpu.VMEM((2 * slots, width), jnp.bfloat16),
        pltpu.VMEM((2 * slots, width), jnp.bfloat16),
        pltpu.VMEM((heads, 2 * slots), jnp.float32),
        pltpu.VMEM((heads, 128), jnp.float32),
        pltpu.VMEM((heads, 128), jnp.float32),
        pltpu.VMEM((slots + 16, width), jnp.bfloat16),
    ]


def fused_kernel(
    grid_rows, token_ref, cell_ref, count_ref, gain_ref, tokens_h, bias_h, lift_h, query_h, key_h,
    value_h, out_h, out_ref, lift_v, query_v, key_v, value_v, out_v, weight_sems, sent, landed,
    cells, rows, tokens_ref, bias_rows, cells_ref, bias_ref, local_sem, tile_send, tile_recv, core_send, core_recv, side_send, side_recv,
    cell_send, cell_recv, *scratch
):
    bevy, bevx, cam = (lax.axis_index(name) for name in ("bevy", "bevx", "cam"))
    count_y, count_x = lax.axis_size("bevy"), lax.axis_size("bevx")
    tiles = count_y * count_x
    me = bevy * count_x + bevx
    block = 2 * SLOTS
    group = count_x * block
    half = sent.shape[1]
    mesh_id = pl.DeviceIdType.MESH
    has_up = bevy > 0
    has_down = bevy < count_y - 1
    has_side = jnp.where(cam == 0, bevy, count_y - 1 - bevy) > 0
    mate = (bevy, bevx, 1 - cam)
    up = (bevy - 1, bevx, 1)
    down = (bevy + 1, bevx, 0)
    across = (bevy + 2 * cam - 1, bevx, 1 - cam)

    row_start = (bevy * 2 + cam) * ROWS_DEV
    tokens_in = pltpu.make_async_copy(tokens_h, tokens_ref, local_sem.at[2])
    tokens_in.start()
    above = jnp.maximum(row_start - HALO, 0)
    below = jnp.minimum(row_start + ROWS_DEV, grid_rows - HALO)
    ranges = [(above, 0, HALO), (row_start, HALO, ROWS_DEV), (below, HALO + ROWS_DEV, HALO)]
    bias_in = [
        pltpu.make_async_copy(
            bias_h.at[pl.ds(first, size)], bias_rows.at[pl.ds(to, size)], local_sem.at[3 + i]
        )
        for i, (first, to, size) in enumerate(ranges)
    ]
    for copy in bias_in:
        copy.start()

    barrier = pltpu.get_barrier_semaphore()

    @pl.loop(1, tiles)
    def _(step):
        peer = (me + step) % tiles
        pl.semaphore_signal(
            barrier, inc=1, device_id=(peer // count_x, peer % count_x, cam), device_id_type=mesh_id
        )

    pl.semaphore_signal(barrier, inc=1, device_id=mate, device_id_type=mesh_id)

    @pl.when(has_side)
    def _():
        pl.semaphore_signal(barrier, inc=1, device_id=across, device_id_type=mesh_id)

    live = lax.broadcasted_iota(jnp.int32, token_ref.shape, 0) < count_ref[...]
    wanted = jnp.where(live, token_ref[...], -1).astype(jnp.bfloat16)
    line = lax.broadcasted_iota(jnp.int32, (sent.shape[0], tiles), 0)
    at_tile = (lax.broadcasted_iota(jnp.int32, line.shape, 1) == line // block).astype(jnp.bfloat16)
    wanted = dot_last(at_tile, wanted)
    line = lax.broadcasted_iota(jnp.int32, wanted.shape, 0)
    at_slot = lax.broadcasted_iota(jnp.int32, wanted.shape, 1) == line % SLOTS
    wanted = jnp.sum(jnp.where(at_slot, wanted, 0.0), axis=1, keepdims=True).astype(jnp.int32)
    lane = lax.broadcasted_iota(jnp.int32, (tiles, tiles * SLOTS), 1)
    at_tile = lane // SLOTS == lax.broadcasted_iota(jnp.int32, lane.shape, 0)
    at_tile = at_tile.astype(jnp.bfloat16)
    high = (cell_ref[...] // 32).astype(jnp.bfloat16)
    low = (cell_ref[...] % 32).astype(jnp.bfloat16)
    high = jnp.dot(high, at_tile, preferred_element_type=jnp.float32)
    low = jnp.dot(low, at_tile, preferred_element_type=jnp.float32)
    lane = lax.broadcasted_iota(jnp.int32, high.shape, 1)
    at_slot = lane % SLOTS == lax.broadcasted_iota(jnp.int32, high.shape, 0)
    line = jnp.sum(jnp.where(at_slot, high * 32.0 + low, 0.0), axis=0, keepdims=True)
    cells_ref[...] = jnp.broadcast_to(line.astype(jnp.int32), cells_ref.shape)
    tokens_in.wait()
    choose = lax.broadcasted_iota(jnp.int32, (wanted.shape[0], tokens_ref.shape[0]), 1) == wanted
    choose = choose.astype(jnp.bfloat16)
    left = jnp.dot(choose, tokens_ref[:, :half], preferred_element_type=jnp.float32)
    right = jnp.dot(choose, tokens_ref[:, half:], preferred_element_type=jnp.float32)
    in_block = lax.broadcasted_iota(jnp.int32, left.shape, 0) % block
    sent[...] = jnp.where(in_block < SLOTS, left, right).astype(jnp.bfloat16)

    pl.semaphore_wait(barrier, tiles + jnp.where(has_side, 1, 0))

    def at(start, size):
        return pl.ds(pl.multiple_of(start, block), size)

    def tile_copy(peer, slot):
        return pltpu.make_async_remote_copy(
            src_ref=sent.at[at(peer * block, block)],
            dst_ref=landed.at[cam, at(slot * block, block)],
            send_sem=tile_send.at[peer],
            recv_sem=tile_recv.at[slot],
            device_id=(peer // count_x, peer % count_x, cam),
            device_id_type=mesh_id,
        )

    @pl.loop(1, tiles)
    def _(step):
        tile_copy((me + step) % tiles, me).start()

    kept = pltpu.make_async_copy(
        sent.at[at(me * block, block)], landed.at[cam, at(me * block, block)], local_sem.at[0]
    )
    kept.start()
    own_cells = pltpu.make_async_copy(cells_ref, cells.at[cam], local_sem.at[1])
    own_cells.start()

    def cell_copy(target, slot, index, source):
        return pltpu.make_async_remote_copy(
            src_ref=cells_ref,
            dst_ref=cells.at[slot],
            send_sem=cell_send.at[index],
            recv_sem=cell_recv.at[slot],
            device_id=target,
            device_id_type=mesh_id,
        )

    def row_copy(target, slot, part, send, recv):
        return pltpu.make_async_remote_copy(
            src_ref=landed.at[cam, at(part * group, group)],
            dst_ref=landed.at[slot, at(part * group, group)],
            send_sem=send,
            recv_sem=recv,
            device_id=target,
            device_id_type=mesh_id,
        )

    def mate_rows(part, slot):
        return row_copy(mate, slot, part, core_send.at[part], core_recv.at[part])

    def side_rows(target, which, part, source):
        return row_copy(
            target, 2 + source, part, side_send.at[which, part], side_recv.at[source, part]
        )

    cell_copy(mate, cam, 0, cam).start()

    @pl.when(has_up)
    def _():
        cell_copy(up, 2 + cam, 1, cam).start()

    @pl.when(has_down)
    def _():
        cell_copy(down, 2 + cam, 2, cam).start()

    pairs = [(lift_h, lift_v), (query_h, query_v), (key_h, key_v), (value_h, value_v), (out_h, out_v)]
    copies = [pltpu.make_async_copy(a, b, weight_sems.at[i]) for i, (a, b) in enumerate(pairs)]
    for copy in copies:
        copy.start()

    for copy in bias_in:
        copy.wait()
    bias_ref[...] = jnp.concatenate([bias_rows[i] for i in range(bias_rows.shape[0])], axis=1)
    own_cells.wait()
    cell_copy(mate, 1 - cam, 0, cam).wait_recv()

    @pl.when(has_side)
    def _():
        cell_copy(across, 2, 0, cam).wait_recv()
        cell_copy(across, 3, 0, cam).wait_recv()

    @pl.when(jnp.logical_not(has_side))
    def _():
        cells[2:] = jnp.zeros_like(cells[2:])
        landed[2:] = jnp.zeros_like(landed[2:])

    slots = rows.shape[0] // 4

    def join_halves(index):
        slot = lax.broadcasted_iota(jnp.int32, (slots, landed.shape[1]), 0)
        row = lax.broadcasted_iota(jnp.int32, (slots, landed.shape[1]), 1)
        first = slot // SLOTS * block + slot % SLOTS
        for side in range(2):
            take = (row == first + side * SLOTS).astype(jnp.bfloat16)
            rows[index * slots : (index + 1) * slots, side * half : (side + 1) * half] = jnp.dot(
                take, landed[index], preferred_element_type=jnp.float32
            ).astype(jnp.bfloat16)

    def wait_for(name):
        if name == "own":
            kept.wait()

            @pl.loop(0, count_y)
            def _(step):
                part = (bevy + step) % count_y

                @pl.loop(0, count_x)
                def _(index):
                    source = part * count_x + index

                    @pl.when(source != me)
                    def _():
                        tile_copy(source, source).wait_recv()

                mate_rows(part, cam).start()

                @pl.when(has_up)
                def _():
                    side_rows(up, 0, part, cam).start()

                @pl.when(has_down)
                def _():
                    side_rows(down, 1, part, cam).start()


            @pl.loop(0, count_y)
            def _(part):
                mate_rows(part, 1 - cam).wait_recv()

            join_halves(0)
            join_halves(1)
            return
        if name == "side":

            @pl.when(has_side)
            def _():
                @pl.loop(0, count_y)
                def _(part):
                    side_rows(across, 0, part, 0).wait_recv()
                    side_rows(across, 0, part, 1).wait_recv()

            join_halves(2)
            join_halves(3)
            return
        for copy in {"lift": copies[:1], "qkv": copies[1:4], "out": copies[4:]}[name]:
            copy.wait()

    cells_own = jnp.concatenate([cells[0, 0:1, :], cells[1, 0:1, :]], axis=1)
    cells_side = jnp.concatenate([cells[2, 0:1, :], cells[3, 0:1, :]], axis=1)
    slot_attention(
        cam, row_start, grid_rows, cells_own, cells_side, rows, bias_ref, gain_ref, lift_v, query_v,
        key_v, value_v, out_v, out_ref, *scratch, wait_for,
    )

    @pl.loop(1, tiles)
    def _(step):
        tile_copy((me + step) % tiles, me).wait_send()

    @pl.loop(0, count_y)
    def _(part):
        mate_rows(part, cam).wait_send()

    cell_copy(mate, cam, 0, cam).wait_send()

    @pl.when(has_up)
    def _():
        cell_copy(up, 2 + cam, 1, cam).wait_send()

        @pl.loop(0, count_y)
        def _(part):
            side_rows(up, 0, part, cam).wait_send()

    @pl.when(has_down)
    def _():
        cell_copy(down, 2 + cam, 2, cam).wait_send()

        @pl.loop(0, count_y)
        def _(part):
            side_rows(down, 1, part, cam).wait_send()


def slot_body(
    image_tokens, lift_weight, route_token, route_cell, slot_counts, norm_gain, w_query, w_key,
    w_value, w_out, key_bias,
):
    tile_count, slot_count = route_token.shape[2:]
    width = lift_weight.shape[1]
    heads = key_bias.shape[2]
    grid_rows = key_bias.shape[0]
    half = image_tokens.shape[1] // 2
    slots = 2 * tile_count * slot_count
    vmem = pl.BlockSpec(memory_space=pltpu.VMEM)
    anywhere = pl.BlockSpec(memory_space=pl.ANY)
    weights = (lift_weight, w_query, w_key, w_value, w_out)
    count_y = lax.axis_size("bevy")
    dma = pltpu.SemaphoreType.DMA
    out = pl.pallas_call(
        functools.partial(fused_kernel, grid_rows),
        out_shape=jax.ShapeDtypeStruct((ROWS_DEV * COLS_DEV, width), jnp.bfloat16),
        in_specs=[vmem] * 4 + [anywhere] * 7,
        out_specs=vmem,
        scratch_shapes=[pltpu.VMEM(w.shape, jnp.bfloat16) for w in weights]
        + [
            dma((5,)),
            pltpu.VMEM((slots, half), jnp.bfloat16),
            pltpu.VMEM((4, slots, half), jnp.bfloat16),
            pltpu.VMEM((4, 8, slots // 2), jnp.int32),
            pltpu.VMEM((2 * slots, 2 * half), jnp.bfloat16),
            pltpu.VMEM(image_tokens.shape, jnp.bfloat16),
            pltpu.VMEM((2 * ROWS_DEV, heads, COLS_DEV), jnp.bfloat16),
            pltpu.VMEM((8, slots // 2), jnp.int32),
            pltpu.VMEM((heads, 2 * ROWS_DEV * COLS_DEV), jnp.bfloat16),
            dma((6,)),
            dma((tile_count,)),
            dma((tile_count,)),
            dma((count_y,)),
            dma((count_y,)),
            dma((2, count_y)),
            dma((2, count_y)),
            dma((3,)),
            dma((4,)),
        ]
        + compute_scratch(slots, heads, width),
        compiler_params=pltpu.CompilerParams(
            vmem_limit_bytes=62 * 2**20, collective_id=0, has_side_effects=True
        ),
    )(
        route_token[0, 0].T,
        route_cell[:, 0, 0, :].T,
        slot_counts.reshape(1, -1),
        norm_gain.reshape(1, -1),
        image_tokens,
        key_bias.transpose(0, 2, 1),
        *weights,
    )
    return out.reshape(ROWS_DEV, COLS_DEV, width)


def solution(mesh):
    placed = (
        P(("bevy", "bevx", "cam"), None),
        P(),
        P(("bevy", "bevx"), "cam", None, None),
        P(None, "cam", ("bevy", "bevx"), None),
        P(("bevy", "bevx"), "cam", None),
        P(),
        P(),
        P(),
        P(),
        P(),
        P(None, "bevx", None),
    )
    tiles = mesh.shape["bevy"] * mesh.shape["bevx"]
    sparse = mesh.shape["cam"] == 2 and tiles <= 16
    return jax.shard_map(
        slot_body if sparse else dense_body,
        mesh=mesh,
        in_specs=placed,
        out_specs=P(("bevy", "cam"), "bevx", None),
        check_vma=False,
    )
```

```python
import functools

import jax
import jax.numpy as jnp
from jax import lax
from jax.experimental import pallas as pl
from jax.experimental.pallas import tpu as pltpu
from jax.sharding import PartitionSpec as P

ROWS_DEV = 8
COLS_DEV = 64
HALO = 4


def extended_2(cells, sides, width):
    for axis, dim in sides:
        count = lax.axis_size(axis)
        ends = count - 1
        head = lax.slice_in_dim(cells, 0, width, axis=dim)
        tail = lax.slice_in_dim(cells, cells.shape[dim] - width, cells.shape[dim], axis=dim)
        cells = jnp.concatenate(
            [
                lax.ppermute(tail, axis, [(i, (i + 1) % count) for i in range(ends)]),
                cells,
                lax.ppermute(head, axis, [((i + 1) % count, i) for i in range(ends)]),
            ],
            axis=dim,
        )
    return cells


def dense_body(
    image_tokens,
    lift_weight,
    route_token,
    route_cell,
    slot_counts,
    norm_gain,
    w_query,
    w_key,
    w_value,
    w_out,
    key_bias,
):
    tile_count = route_token.shape[2]
    slot_count = route_token.shape[3]
    width_out = lift_weight.shape[1]
    head_count = key_bias.shape[2]
    head_size = width_out // head_count
    grid_rows = key_bias.shape[0]
    own_cells = ROWS_DEV * COLS_DEV
    is_live = (
        lax.broadcasted_iota(jnp.int32, (tile_count, slot_count), 1) < slot_counts[0, 0][:, None]
    )
    token_index = route_token[0, 0]
    projected = jnp.dot(image_tokens, lift_weight, preferred_element_type=jnp.float32).astype(
        jnp.bfloat16
    )
    picked = jnp.where(is_live[:, :, None], projected[token_index], jnp.zeros((), jnp.bfloat16))
    arrived = lax.all_to_all(picked, ("bevy", "bevx"), split_axis=0, concat_axis=0, tiled=True)
    arrived_rows = arrived.reshape(tile_count * slot_count, -1)
    cell_index = route_cell[:, 0, 0, :].reshape(-1)
    both_rows, both_cells = (
        lax.all_gather(arrived_rows, "cam", axis=0, tiled=True),
        lax.all_gather(cell_index, "cam", axis=0, tiled=True),
    )
    first_cell = lax.axis_index("cam") * own_cells
    cell_ids = first_cell + lax.broadcasted_iota(jnp.int32, (own_cells, both_cells.shape[0]), 0)
    one_hot = (cell_ids == both_cells[None, :]).astype(jnp.bfloat16)
    lifted = jnp.dot(one_hot, both_rows, preferred_element_type=jnp.float32)
    mean_square = jnp.mean(lifted * lifted, axis=-1, keepdims=True)
    normed = (lifted * lax.rsqrt(mean_square + 1e-06) * norm_gain).astype(jnp.bfloat16)
    queries = jnp.dot(normed, w_query, preferred_element_type=jnp.float32).astype(jnp.bfloat16)
    row_start = lax.axis_index(("bevy", "cam")) * ROWS_DEV
    key_local = jnp.dot(normed, w_key, preferred_element_type=jnp.float32).astype(jnp.bfloat16)
    value_local = jnp.dot(normed, w_value, preferred_element_type=jnp.float32).astype(jnp.bfloat16)
    stacked = jnp.concatenate([key_local, value_local], axis=-1).reshape(
        ROWS_DEV, COLS_DEV, 2 * width_out
    )
    extended = extended_2(stacked, ((("bevy", "cam"), 0),), HALO).reshape(-1, 2 * width_out)
    key_vectors = extended[:, :width_out]
    value_vectors = extended[:, width_out:]
    bias_padded = jnp.pad(key_bias, ((HALO, HALO), (0, 0), (0, 0)))
    bias_rows = (
        lax.dynamic_slice_in_dim(bias_padded, row_start, 2 * ROWS_DEV, 0)
        .reshape(-1, head_count)
        .astype(jnp.float32)
    )
    key_row = row_start - HALO + jnp.arange(2 * ROWS_DEV, dtype=jnp.int32)
    key_valid = jnp.repeat((key_row >= 0) & (key_row < grid_rows), COLS_DEV)
    query_heads = queries.reshape(own_cells, head_count, head_size)
    key_heads = key_vectors.reshape(-1, head_count, head_size)
    value_heads = value_vectors.reshape(-1, head_count, head_size)
    score_scale = head_size ** (-0.5)
    scores = (
        jnp.einsum("qhd,khd->hqk", query_heads, key_heads, preferred_element_type=jnp.float32)
        * score_scale
    )
    scores = scores + bias_rows.T[:, None, :]
    scores = jnp.where(key_valid[None, None, :], scores, -jnp.inf)
    top_score = jnp.max(scores, axis=-1, keepdims=True)
    expo = jnp.exp(scores - top_score)
    weights = (expo / jnp.sum(expo, axis=-1, keepdims=True)).astype(jnp.bfloat16)
    attended = jnp.einsum(
        "hqk,khd->qhd", weights, value_heads, preferred_element_type=jnp.float32
    ).astype(jnp.bfloat16)
    attended = attended.reshape(own_cells, width_out)
    result = lifted + jnp.dot(attended, w_out, preferred_element_type=jnp.float32)
    return result.astype(jnp.bfloat16).reshape(ROWS_DEV, COLS_DEV, width_out)


COL_TILE = 256
NEVER = -1e30
SLOTS = 8


def to_column(row):
    size = row.shape[1]
    across = lax.broadcasted_iota(jnp.int32, (size, size), 1)
    down = lax.broadcasted_iota(jnp.int32, (size, size), 0)
    return jnp.sum(jnp.where(across == down, row, 0), axis=1, keepdims=True)


def dot_last(left, right):
    return lax.dot_general(
        left, right, (((1,), (1,)), ((), ())), preferred_element_type=jnp.float32
    )


def slot_masks(cells, shift, exists, window):
    size = cells.shape[1]
    column = to_column(cells)
    same = column == cells
    down = lax.broadcasted_iota(jnp.int32, (size, size), 0)
    across = lax.broadcasted_iota(jnp.int32, (size, size), 1)
    repeat_row = jnp.sum(jnp.where(same & (down < across), 1, 0), axis=0, keepdims=True)
    repeat_col = jnp.sum(jnp.where(same & (across < down), 1, 0), axis=1, keepdims=True)

    def place(cell, repeat):
        spot = cell + shift
        keep = (repeat == 0) & (spot >= 0) & (spot < window) & exists
        return jnp.where(keep, spot, -1)

    return same.astype(jnp.bfloat16), place(cells, repeat_row), place(column, repeat_col)


def slot_attention(
    cam,
    row_start,
    grid_rows,
    cells_own,
    cells_side,
    rows_ref,
    bias_ref,
    gain_ref,
    lift_ref,
    query_w,
    key_w,
    value_w,
    out_w,
    out_ref,
    lifted,
    normed,
    queries,
    keys,
    values,
    key_extra,
    rest_top,
    rest_sum,
    attended,
    wait_for,
):
    slots = cells_own.shape[1]
    heads, window = bias_ref.shape
    width = lifted.shape[1]
    head_size = width // heads
    own_cells = ROWS_DEV * COLS_DEV
    tile_rows = 2 * ROWS_DEV
    halo_cells = HALO * COLS_DEV
    side_shift = (tile_rows - HALO) * COLS_DEV
    own_same, own_row, own_col = slot_masks(
        cells_own, halo_cells - cam * own_cells, True, window
    )
    side_exists = jnp.where(cam == 0, row_start > 0, row_start + ROWS_DEV < grid_rows)
    side_same, side_row, side_col = slot_masks(
        cells_side, jnp.where(cam == 0, -side_shift, side_shift), side_exists, window
    )
    spot_row = jnp.concatenate([own_row, side_row], axis=1)
    spot_col = jnp.concatenate([own_col, side_col], axis=0)
    hit = lax.broadcasted_iota(jnp.int32, (2 * slots, window), 1) == spot_col
    taken = jnp.max(jnp.where(hit, 1.0, 0.0), axis=0, keepdims=True) > 0.5
    bias = bias_ref[...]
    extra = dot_last(bias, hit.astype(jnp.bfloat16))
    extra = jnp.where(spot_row >= 0, extra, NEVER)
    key_extra[...] = extra
    window_row = row_start - HALO + lax.broadcasted_iota(jnp.int32, (1, window), 1) // COLS_DEV
    empty = jnp.logical_not(taken) & (window_row >= 0) & (window_row < grid_rows)
    rest = jnp.where(empty, bias.astype(jnp.float32), NEVER)
    top = jnp.max(rest, axis=1, keepdims=True)
    total = jnp.sum(jnp.where(empty, jnp.exp(rest - top), 0.0), axis=1, keepdims=True)
    rest_top[...] = jnp.broadcast_to(top, rest_top.shape)
    rest_sum[...] = jnp.broadcast_to(total, rest_sum.shape)

    def lift_group(group, same):
        part = pl.ds(group * slots, slots)

        @pl.loop(0, width // COL_TILE)
        def _(step):
            cols = pl.ds(pl.multiple_of(step * COL_TILE, COL_TILE), COL_TILE)
            made = jnp.dot(rows_ref[part, :], lift_ref[:, cols], preferred_element_type=jnp.float32)
            lifted[part, cols] = jnp.dot(
                same, made.astype(jnp.bfloat16), preferred_element_type=jnp.float32
            )

        whole = lifted[part, :]
        mean_square = jnp.mean(whole * whole, axis=-1, keepdims=True)
        normed[part, :] = (whole * lax.rsqrt(mean_square + 1e-06) * gain_ref[...]).astype(
            jnp.bfloat16
        )

    def key_group(group):
        part = pl.ds(group * slots, slots)

        @pl.loop(0, width // COL_TILE)
        def _(step):
            cols = pl.ds(pl.multiple_of(step * COL_TILE, COL_TILE), COL_TILE)
            if group == 0:
                made = jnp.dot(
                    normed[part, :], query_w[:, cols], preferred_element_type=jnp.float32
                ).astype(jnp.bfloat16)
                queries[:, cols] = made * jnp.asarray(head_size**-0.5, jnp.bfloat16)
            keys[part, cols] = jnp.dot(
                normed[part, :], key_w[:, cols], preferred_element_type=jnp.float32
            ).astype(jnp.bfloat16)
            values[part, cols] = jnp.dot(
                normed[part, :], value_w[:, cols], preferred_element_type=jnp.float32
            ).astype(jnp.bfloat16)

    wait_for("own")
    wait_for("lift")
    lift_group(0, own_same)
    wait_for("qkv")
    key_group(0)
    wait_for("side")
    lift_group(1, side_same)
    key_group(1)

    blank_top = jnp.maximum(jnp.max(extra, axis=1, keepdims=True), top)
    blank = jnp.exp(extra - blank_top)
    blank_sum = jnp.sum(blank, axis=1, keepdims=True) + total * jnp.exp(top - blank_top)
    blank = (blank / blank_sum).astype(jnp.bfloat16)
    blank = jnp.dot(blank, values[...], preferred_element_type=jnp.float32)
    lane_head = lax.broadcasted_iota(jnp.int32, (heads, width), 1) // head_size
    own_head = lax.broadcasted_iota(jnp.int32, (heads, width), 0) == lane_head
    blank = jnp.sum(jnp.where(own_head, blank, 0.0), axis=0, keepdims=True)
    attended[slots:, :] = jnp.broadcast_to(blank, (16, width)).astype(jnp.bfloat16)

    low = lax.broadcasted_iota(jnp.int32, (slots, 2 * head_size), 1) < head_size

    @pl.loop(0, heads // 16)
    def _(step):
        for inner in range(8):
            pair = step * 8 + inner
            cols = pl.ds(pl.multiple_of(pair * 2 * head_size, 2 * head_size), 2 * head_size)
            query = queries[:, cols]
            parts = []
            for side in range(2):
                head = pl.ds(pair * 2 + side, 1)
                mine = low if side == 0 else jnp.logical_not(low)
                score = dot_last(jnp.where(mine, query, jnp.zeros_like(query)), keys[:, cols])
                score = score + key_extra[head, :]
                rest_best = rest_top[head, :][:, :1]
                best = jnp.maximum(jnp.max(score, axis=1, keepdims=True), rest_best)
                expo = jnp.exp(score - best)
                weight_sum = jnp.sum(expo, axis=1, keepdims=True)
                weight_sum = weight_sum + rest_sum[head, :][:, :1] * jnp.exp(rest_best - best)
                mixed = jnp.dot(
                    expo.astype(jnp.bfloat16), values[:, cols], preferred_element_type=jnp.float32
                )
                parts.append(mixed / weight_sum)
            attended[:slots, cols] = jnp.where(low, parts[0], parts[1]).astype(jnp.bfloat16)

    cell = lax.broadcasted_iota(jnp.int32, (own_cells, slots), 0) + halo_cells
    spread = cell == own_row
    filled = jnp.max(jnp.where(spread, 1.0, 0.0), axis=1, keepdims=True) > 0.5
    spread = spread.astype(jnp.bfloat16)

    wait_for("out")

    @pl.loop(0, width // COL_TILE)
    def _(step):
        cols = pl.ds(pl.multiple_of(step * COL_TILE, COL_TILE), COL_TILE)
        mixed = jnp.dot(attended[...], out_w[:, cols], preferred_element_type=jnp.float32)
        final = (lifted[:slots, cols] + mixed[:slots]).astype(jnp.bfloat16)
        placed = jnp.dot(spread, final, preferred_element_type=jnp.float32)
        out_ref[:, cols] = jnp.where(filled, placed, mixed[slots : slots + 1]).astype(jnp.bfloat16)


def compute_scratch(slots, heads, width):
    return [
        pltpu.VMEM((2 * slots, width), jnp.float32),
        pltpu.VMEM((2 * slots, width), jnp.bfloat16),
        pltpu.VMEM((slots, width), jnp.bfloat16),
        pltpu.VMEM((2 * slots, width), jnp.bfloat16),
        pltpu.VMEM((2 * slots, width), jnp.bfloat16),
        pltpu.VMEM((heads, 2 * slots), jnp.float32),
        pltpu.VMEM((heads, 128), jnp.float32),
        pltpu.VMEM((heads, 128), jnp.float32),
        pltpu.VMEM((slots + 16, width), jnp.bfloat16),
    ]


def fused_kernel(
    grid_rows, token_ref, cell_ref, count_ref, gain_ref, tokens_h, bias_h, lift_h, query_h, key_h,
    value_h, out_h, out_ref, lift_v, query_v, key_v, value_v, out_v, weight_sems, sent, landed,
    cells, rows, tokens_ref, bias_rows, cells_ref, bias_ref, local_sem, tile_send, tile_recv, core_send, core_recv, side_send, side_recv,
    cell_send, cell_recv, *scratch
):
    bevy, bevx, cam = (lax.axis_index(name) for name in ("bevy", "bevx", "cam"))
    count_y, count_x = lax.axis_size("bevy"), lax.axis_size("bevx")
    tiles = count_y * count_x
    me = bevy * count_x + bevx
    block = 2 * SLOTS
    group = count_x * block
    half = sent.shape[1]
    mesh_id = pl.DeviceIdType.MESH
    has_up = bevy > 0
    has_down = bevy < count_y - 1
    has_side = jnp.where(cam == 0, bevy, count_y - 1 - bevy) > 0
    mate = (bevy, bevx, 1 - cam)
    up = (bevy - 1, bevx, 1)
    down = (bevy + 1, bevx, 0)
    across = (bevy + 2 * cam - 1, bevx, 1 - cam)

    row_start = (bevy * 2 + cam) * ROWS_DEV
    tokens_in = pltpu.make_async_copy(tokens_h, tokens_ref, local_sem.at[2])
    tokens_in.start()
    above = jnp.maximum(row_start - HALO, 0)
    below = jnp.minimum(row_start + ROWS_DEV, grid_rows - HALO)
    ranges = [(above, 0, HALO), (row_start, HALO, ROWS_DEV), (below, HALO + ROWS_DEV, HALO)]
    bias_in = [
        pltpu.make_async_copy(
            bias_h.at[pl.ds(first, size)], bias_rows.at[pl.ds(to, size)], local_sem.at[3 + i]
        )
        for i, (first, to, size) in enumerate(ranges)
    ]
    for copy in bias_in:
        copy.start()

    barrier = pltpu.get_barrier_semaphore()

    @pl.loop(1, tiles)
    def _(step):
        peer = (me + step) % tiles
        pl.semaphore_signal(
            barrier, inc=1, device_id=(peer // count_x, peer % count_x, cam), device_id_type=mesh_id
        )

    pl.semaphore_signal(barrier, inc=1, device_id=mate, device_id_type=mesh_id)

    @pl.when(has_side)
    def _():
        pl.semaphore_signal(barrier, inc=1, device_id=across, device_id_type=mesh_id)

    live = lax.broadcasted_iota(jnp.int32, token_ref.shape, 0) < count_ref[...]
    wanted = jnp.where(live, token_ref[...], -1).astype(jnp.bfloat16)
    line = lax.broadcasted_iota(jnp.int32, (sent.shape[0], tiles), 0)
    at_tile = (lax.broadcasted_iota(jnp.int32, line.shape, 1) == line // block).astype(jnp.bfloat16)
    wanted = dot_last(at_tile, wanted)
    line = lax.broadcasted_iota(jnp.int32, wanted.shape, 0)
    at_slot = lax.broadcasted_iota(jnp.int32, wanted.shape, 1) == line % SLOTS
    wanted = jnp.sum(jnp.where(at_slot, wanted, 0.0), axis=1, keepdims=True).astype(jnp.int32)
    lane = lax.broadcasted_iota(jnp.int32, (tiles, tiles * SLOTS), 1)
    at_tile = lane // SLOTS == lax.broadcasted_iota(jnp.int32, lane.shape, 0)
    at_tile = at_tile.astype(jnp.bfloat16)
    high = (cell_ref[...] // 32).astype(jnp.bfloat16)
    low = (cell_ref[...] % 32).astype(jnp.bfloat16)
    high = jnp.dot(high, at_tile, preferred_element_type=jnp.float32)
    low = jnp.dot(low, at_tile, preferred_element_type=jnp.float32)
    lane = lax.broadcasted_iota(jnp.int32, high.shape, 1)
    at_slot = lane % SLOTS == lax.broadcasted_iota(jnp.int32, high.shape, 0)
    line = jnp.sum(jnp.where(at_slot, high * 32.0 + low, 0.0), axis=0, keepdims=True)
    cells_ref[...] = jnp.broadcast_to(line.astype(jnp.int32), cells_ref.shape)
    tokens_in.wait()
    choose = lax.broadcasted_iota(jnp.int32, (wanted.shape[0], tokens_ref.shape[0]), 1) == wanted
    choose = choose.astype(jnp.bfloat16)
    left = jnp.dot(choose, tokens_ref[:, :half], preferred_element_type=jnp.float32)
    right = jnp.dot(choose, tokens_ref[:, half:], preferred_element_type=jnp.float32)
    in_block = lax.broadcasted_iota(jnp.int32, left.shape, 0) % block
    sent[...] = jnp.where(in_block < SLOTS, left, right).astype(jnp.bfloat16)

    pl.semaphore_wait(barrier, tiles + jnp.where(has_side, 1, 0))

    def at(start, size):
        return pl.ds(pl.multiple_of(start, block), size)

    def tile_copy(peer, slot):
        return pltpu.make_async_remote_copy(
            src_ref=sent.at[at(peer * block, block)],
            dst_ref=landed.at[cam, at(slot * block, block)],
            send_sem=tile_send.at[peer],
            recv_sem=tile_recv.at[slot],
            device_id=(peer // count_x, peer % count_x, cam),
            device_id_type=mesh_id,
        )

    @pl.loop(1, tiles)
    def _(step):
        tile_copy((me + step) % tiles, me).start()

    kept = pltpu.make_async_copy(
        sent.at[at(me * block, block)], landed.at[cam, at(me * block, block)], local_sem.at[0]
    )
    kept.start()
    own_cells = pltpu.make_async_copy(cells_ref, cells.at[cam], local_sem.at[1])
    own_cells.start()

    def cell_copy(target, slot, index, source):
        return pltpu.make_async_remote_copy(
            src_ref=cells_ref,
            dst_ref=cells.at[slot],
            send_sem=cell_send.at[index],
            recv_sem=cell_recv.at[slot],
            device_id=target,
            device_id_type=mesh_id,
        )

    def row_copy(target, slot, part, send, recv):
        return pltpu.make_async_remote_copy(
            src_ref=landed.at[cam, at(part * group, group)],
            dst_ref=landed.at[slot, at(part * group, group)],
            send_sem=send,
            recv_sem=recv,
            device_id=target,
            device_id_type=mesh_id,
        )

    def mate_rows(part, slot):
        return row_copy(mate, slot, part, core_send.at[part], core_recv.at[part])

    def side_rows(target, which, part, source):
        return row_copy(
            target, 2 + source, part, side_send.at[which, part], side_recv.at[source, part]
        )

    cell_copy(mate, cam, 0, cam).start()

    @pl.when(has_up)
    def _():
        cell_copy(up, 2 + cam, 1, cam).start()

    @pl.when(has_down)
    def _():
        cell_copy(down, 2 + cam, 2, cam).start()

    pairs = [(lift_h, lift_v), (query_h, query_v), (key_h, key_v), (value_h, value_v), (out_h, out_v)]
    copies = [pltpu.make_async_copy(a, b, weight_sems.at[i]) for i, (a, b) in enumerate(pairs)]
    for copy in copies:
        copy.start()

    for copy in bias_in:
        copy.wait()
    bias_ref[...] = jnp.concatenate([bias_rows[i] for i in range(bias_rows.shape[0])], axis=1)
    own_cells.wait()
    cell_copy(mate, 1 - cam, 0, cam).wait_recv()

    @pl.when(has_side)
    def _():
        cell_copy(across, 2, 0, cam).wait_recv()
        cell_copy(across, 3, 0, cam).wait_recv()

    @pl.when(jnp.logical_not(has_side))
    def _():
        cells[2:] = jnp.zeros_like(cells[2:])
        landed[2:] = jnp.zeros_like(landed[2:])

    slots = rows.shape[0] // 4

    def join_halves(index):
        slot = lax.broadcasted_iota(jnp.int32, (slots, landed.shape[1]), 0)
        row = lax.broadcasted_iota(jnp.int32, (slots, landed.shape[1]), 1)
        first = slot // SLOTS * block + slot % SLOTS
        for side in range(2):
            take = (row == first + side * SLOTS).astype(jnp.bfloat16)
            rows[index * slots : (index + 1) * slots, side * half : (side + 1) * half] = jnp.dot(
                take, landed[index], preferred_element_type=jnp.float32
            ).astype(jnp.bfloat16)

    def wait_for(name):
        if name == "own":
            kept.wait()

            @pl.loop(0, count_y)
            def _(step):
                part = (bevy + step) % count_y

                @pl.loop(0, count_x)
                def _(index):
                    source = part * count_x + index

                    @pl.when(source != me)
                    def _():
                        tile_copy(source, source).wait_recv()

                mate_rows(part, cam).start()

                @pl.when(has_up)
                def _():
                    side_rows(up, 0, part, cam).start()

                @pl.when(has_down)
                def _():
                    side_rows(down, 1, part, cam).start()


            @pl.loop(0, count_y)
            def _(part):
                mate_rows(part, 1 - cam).wait_recv()

            join_halves(0)
            join_halves(1)
            return
        if name == "side":

            @pl.when(has_side)
            def _():
                @pl.loop(0, count_y)
                def _(part):
                    side_rows(across, 0, part, 0).wait_recv()
                    side_rows(across, 0, part, 1).wait_recv()

            join_halves(2)
            join_halves(3)
            return
        for copy in {"lift": copies[:1], "qkv": copies[1:4], "out": copies[4:]}[name]:
            copy.wait()

    cells_own = jnp.concatenate([cells[0, 0:1, :], cells[1, 0:1, :]], axis=1)
    cells_side = jnp.concatenate([cells[2, 0:1, :], cells[3, 0:1, :]], axis=1)
    slot_attention(
        cam, row_start, grid_rows, cells_own, cells_side, rows, bias_ref, gain_ref, lift_v, query_v,
        key_v, value_v, out_v, out_ref, *scratch, wait_for,
    )

    @pl.loop(1, tiles)
    def _(step):
        tile_copy((me + step) % tiles, me).wait_send()

    @pl.loop(0, count_y)
    def _(part):
        mate_rows(part, cam).wait_send()

    cell_copy(mate, cam, 0, cam).wait_send()

    @pl.when(has_up)
    def _():
        cell_copy(up, 2 + cam, 1, cam).wait_send()

        @pl.loop(0, count_y)
        def _(part):
            side_rows(up, 0, part, cam).wait_send()

    @pl.when(has_down)
    def _():
        cell_copy(down, 2 + cam, 2, cam).wait_send()

        @pl.loop(0, count_y)
        def _(part):
            side_rows(down, 1, part, cam).wait_send()


def slot_body(
    image_tokens, lift_weight, route_token, route_cell, slot_counts, norm_gain, w_query, w_key,
    w_value, w_out, key_bias,
):
    tile_count, slot_count = route_token.shape[2:]
    width = lift_weight.shape[1]
    heads = key_bias.shape[2]
    grid_rows = key_bias.shape[0]
    half = image_tokens.shape[1] // 2
    slots = 2 * tile_count * slot_count
    vmem = pl.BlockSpec(memory_space=pltpu.VMEM)
    anywhere = pl.BlockSpec(memory_space=pl.ANY)
    weights = (lift_weight, w_query, w_key, w_value, w_out)
    count_y = lax.axis_size("bevy")
    dma = pltpu.SemaphoreType.DMA
    out = pl.pallas_call(
        functools.partial(fused_kernel, grid_rows),
        out_shape=jax.ShapeDtypeStruct((ROWS_DEV * COLS_DEV, width), jnp.bfloat16),
        in_specs=[vmem] * 4 + [anywhere] * 7,
        out_specs=vmem,
        scratch_shapes=[pltpu.VMEM(w.shape, jnp.bfloat16) for w in weights]
        + [
            dma((5,)),
            pltpu.VMEM((slots, half), jnp.bfloat16),
            pltpu.VMEM((4, slots, half), jnp.bfloat16),
            pltpu.VMEM((4, 8, slots // 2), jnp.int32),
            pltpu.VMEM((2 * slots, 2 * half), jnp.bfloat16),
            pltpu.VMEM(image_tokens.shape, jnp.bfloat16),
            pltpu.VMEM((2 * ROWS_DEV, heads, COLS_DEV), jnp.bfloat16),
            pltpu.VMEM((8, slots // 2), jnp.int32),
            pltpu.VMEM((heads, 2 * ROWS_DEV * COLS_DEV), jnp.bfloat16),
            dma((6,)),
            dma((tile_count,)),
            dma((tile_count,)),
            dma((count_y,)),
            dma((count_y,)),
            dma((2, count_y)),
            dma((2, count_y)),
            dma((3,)),
            dma((4,)),
        ]
        + compute_scratch(slots, heads, width),
        compiler_params=pltpu.CompilerParams(
            vmem_limit_bytes=62 * 2**20, collective_id=0, has_side_effects=True
        ),
    )(
        route_token[0, 0].T,
        route_cell[:, 0, 0, :].T,
        slot_counts.reshape(1, -1),
        norm_gain.reshape(1, -1),
        image_tokens,
        key_bias.transpose(0, 2, 1),
        *weights,
    )
    return out.reshape(ROWS_DEV, COLS_DEV, width)


def solution(mesh):
    placed = (
        P(("bevy", "bevx", "cam"), None),
        P(),
        P(("bevy", "bevx"), "cam", None, None),
        P(None, "cam", ("bevy", "bevx"), None),
        P(("bevy", "bevx"), "cam", None),
        P(),
        P(),
        P(),
        P(),
        P(),
        P(None, "bevx", None),
    )
    tiles = mesh.shape["bevy"] * mesh.shape["bevx"]
    sparse = mesh.shape["cam"] == 2 and tiles <= 16
    return jax.shard_map(
        slot_body if sparse else dense_body,
        mesh=mesh,
        in_specs=placed,
        out_specs=P(("bevy", "cam"), "bevx", None),
        check_vma=False,
    )
```
